128 devices in a mesh: psg: 16 (over y, x), tp: 2 (over core), pb: 4 (over z).
Axes of the slice: x: 4, y: 4, z: 4, core: 2. Of those that a mesh axis runs over, the one named last changes fastest.
Arguments:
- tokens: bfloat16 [4, 32, 256, 4096], P('pb', 'psg', None, 'tp'), may hold values from -6 to 6
- lengths: int32 [4, 32], P('pb'), may hold values from 1 to 256, 5120 in all within a row
- enc_gain: float32 [4096], replicated, may hold values from 0.1 to 1.9
- w_query: bfloat16 [4096, 2048], P(None, 'tp'), may hold values from -1 to 1
- w_key: bfloat16 [4096, 2048], P(None, 'tp'), may hold values from -1 to 1
- w_value: bfloat16 [4096, 2048], P(None, 'tp'), may hold values from -0.09375 to 0.09375
- w_out: bfloat16 [2048, 4096], P('tp'), may hold values from -0.125 to 0.125
- final_gain: float32 [4096], replicated, may hold values from 0.1 to 1.9
- cross_key: bfloat16 [4096, 2048], P(None, 'tp'), may hold values from -1 to 1
- cross_value: bfloat16 [4096, 2048], P(None, 'tp'), may hold values from -0.09375 to 0.09375
- beam_states: bfloat16 [4, 4, 4096], P('pb'), may hold values from -6 to 6
- parents: int32 [4, 4], P('pb'), may hold values from 0 to 3
- dec_gain: float32 [4096], replicated, may hold values from 0.1 to 1.9
- dec_query: bfloat16 [4096, 2048], P('pb', 'tp'), may hold values from -1 to 1
Outputs:
- encoded: bfloat16 [4, 32, 256, 4096], P('pb', 'psg', None, 'tp')
- context: float32 [4, 4, 2048], P('pb', None, 'tp')
The draws below stay inside these ranges and needn't reach their ends.
Inputs may be any that keep to these rules, and one draw needn't show every extreme that they name: The 32 lengths of each question sum to 5120; in each question some passage has length 256.
All inputs are finite; a program needn't handle non-finite values.
Results may differ from the reference program's by a relative error of at most 0.007.
Values may be sent and summed in bfloat16 or wider, within the bound.
A program may use at most 256 MiB of HBM per device.

```python
import math
import jax
import jax.numpy as jnp
import numpy as np
from jax import lax

D = 4096
HEADS = 32
DH = 64
L = 256
BEAMS = 4
PASSAGES = 32
NQ = 4
LIVE = 5120


def shared_direction(key):
    sign_key = jax.random.fold_in(key, 101)
    return (2 * jax.random.randint(sign_key, (D,), 0, 2) - 1).astype(jnp.float32)


def head_pattern(key, label):
    pattern_key = jax.random.fold_in(key, label)
    ranking = jax.random.permutation(jax.random.fold_in(pattern_key, 1), HEADS)
    strong = max(HEADS // 4, 1)
    levels = jnp.where(ranking < strong, 100.0 + 200.0 * ranking.astype(jnp.float32) / max(strong - 1, 1), 0.0)
    strength = jnp.sqrt(8.0 * levels / (0.9 * DH))
    head_signs = (2 * jax.random.randint(jax.random.fold_in(pattern_key, 2), (HEADS, DH), 0, 2) - 1).astype(jnp.float32)
    return (strength[:, None] * head_signs).reshape(HEADS * DH)


def drawn_weight(direction, pattern, jitter):
    return jitter * D ** (-0.5) + direction[:, None] * pattern[None, :] / D


def draw_w_query(key, part):
    direction = shared_direction(key)
    pattern = head_pattern(key, 7)
    key = jax.random.fold_in(key, 11)
    jitter = jnp.clip(jax.random.normal(key, (D, HEADS * DH), jnp.float32), -4.0, 4.0)
    return drawn_weight(direction, pattern, jitter).astype(jnp.bfloat16)


def draw_w_key(key, part):
    direction = shared_direction(key)
    pattern = head_pattern(key, 7)
    key = jax.random.fold_in(key, 12)
    jitter = jnp.clip(jax.random.normal(key, (D, HEADS * DH), jnp.float32), -4.0, 4.0)
    return drawn_weight(direction, pattern, jitter).astype(jnp.bfloat16)


def draw_cross_key(key, part):
    direction = shared_direction(key)
    pattern = head_pattern(key, 8)
    key = jax.random.fold_in(key, 13)
    jitter = jnp.clip(jax.random.normal(key, (D, HEADS * DH), jnp.float32), -4.0, 4.0)
    return drawn_weight(direction, pattern, jitter).astype(jnp.bfloat16)


def draw_dec_query(key, part):
    direction = shared_direction(key)
    pattern = head_pattern(key, 8)
    key = jax.random.fold_in(key, 14)
    jitter = jnp.clip(jax.random.normal(key, (D, HEADS * DH), jnp.float32), -4.0, 4.0)
    return drawn_weight(direction, pattern, jitter).astype(jnp.bfloat16)


def column_scales(low, high):
    position = jnp.arange(D, dtype=jnp.float32) / max(D - 1, 1)
    return jnp.exp(math.log(low) + (math.log(high) - math.log(low)) * position)


def draw_tokens(key, part):
    direction = shared_direction(key)
    key = jax.random.fold_in(key, 15)
    picked = jax.random.randint(jax.random.fold_in(key, 1), (NQ, PASSAGES, L), 0, 16)
    position = jnp.arange(L, dtype=jnp.int32)[None, None, :]
    aligned = (picked == 0) | (position == 0)
    noise_key = jax.random.fold_in(key, 2)
    jitter = jnp.clip(jax.random.normal(noise_key, (NQ, PASSAGES, L, D), jnp.float32), -6.0, 6.0)
    background = jitter
    strength = 3.0
    columns = column_scales(0.5, 2.0)
    foreground = strength * direction + 0.5 * jnp.clip(jitter, -4.0, 4.0)
    mixed = jnp.where(aligned[..., None], foreground, background) * columns
    return jnp.clip(mixed, -6.0, 6.0).astype(jnp.bfloat16)


def draw_beam_states(key, part):
    direction = shared_direction(key)
    key = jax.random.fold_in(key, 16)
    picked = jax.random.randint(jax.random.fold_in(key, 1), (NQ, BEAMS), 0, 2)
    aligned = picked == 0
    noise_key = jax.random.fold_in(key, 2)
    jitter = jnp.clip(jax.random.normal(noise_key, (NQ, BEAMS, D), jnp.float32), -6.0, 6.0)
    background = jitter
    strength = 3.0
    foreground = strength * direction + 0.5 * jnp.clip(jitter, -4.0, 4.0)
    return jnp.where(aligned[..., None], foreground, background).astype(jnp.bfloat16)


def touch_ends(values, own_key, smallest, largest):
    shape = values.shape
    place = [jax.random.randint(jax.random.fold_in(own_key, axis), (), 0, shape[axis]) for axis in range(len(shape))]
    values = values.at[tuple(place)].set(smallest)
    longest = shape.index(max(shape))
    place[longest] = (place[longest] + 1) % shape[longest]
    return values.at[tuple(place)].set(largest)


def block_levels(own_key, dims, shards, least, largest):
    loudness, own = 1.0, jax.random.fold_in(own_key, 6)
    for dim, shards_of in shards:
        steps = jnp.exp(jax.random.uniform(jax.random.fold_in(own, dim), (shards_of,), jnp.float32, least / len(shards), largest / len(shards)))
        loudness = loudness * jnp.repeat(steps, dims[dim] // shards_of).reshape([-1 if axis == dim else 1 for axis in range(len(dims))])
    return loudness


def profile(number_of, total, reach, slope):
    loads = [(1 << 20) // math.isqrt(rank ** slope) + 1 for rank in range(2, number_of + 1)]
    spare, given = total - reach - (number_of - 1), [1] * (number_of - 1)
    while spare > 0:
        movable = [i for i in range(number_of - 1) if given[i] < reach]
        whole, remaining = sum([loads[i] for i in movable]), spare
        for i in movable:
            extra = min(reach - given[i], max(1, remaining * loads[i] // whole), spare)
            given[i] = given[i] + extra
            spare = spare - extra
    return np.array([reach] + given)


def ragged(rng, number_of, total, bound, skew):
    if number_of == 2:
        one = jax.random.randint(rng, (), max(1, total - bound), min(bound, total - 1) + 1)
        return jnp.stack([one, total - one])
    tallies = jnp.asarray(profile(number_of, total, bound, skew), jnp.int32)
    pairs = (number_of - 1) // 2
    giver, sink = tallies[1:1 + 2 * pairs:2], tallies[2:2 + 2 * pairs:2]
    slack = jnp.minimum(giver - 1, bound - sink)
    shifted = jax.random.randint(jax.random.fold_in(rng, 1), (pairs,), 0, 1 << 20) % (slack + 1)
    tallies = tallies.at[1:1 + 2 * pairs:2].set(giver - shifted).at[2:2 + 2 * pairs:2].set(sink + shifted)
    return tallies[jax.random.permutation(jax.random.fold_in(rng, 2), number_of)]


def normal_values(own_key, shape, spread, reach, cuts=(), kind=jnp.bfloat16):
    values = spread * jax.random.normal(own_key, shape, jnp.float32)
    if cuts:
        values = values * block_levels(own_key, shape, cuts, -0.22, 0.18)
    return jnp.clip(values, -reach, reach).astype(kind)


def setup_inputs(seed: int = 0) -> dict:
    streams_of = jax.random.split(jax.random.key(seed), 15)
    return {
        "tokens": draw_tokens(jax.random.fold_in(streams_of[14], 71), 0),
        "lengths": jax.vmap(lambda own: ragged(own, PASSAGES, LIVE, L, 2))(jax.random.split(streams_of[1], NQ)).reshape((NQ, PASSAGES)).astype(jnp.int32),
        "enc_gain": jnp.clip(1.0 + 0.18 * jax.random.normal(streams_of[2], (D,), jnp.float32), 0.1, 1.9),
        "w_query": draw_w_query(jax.random.fold_in(streams_of[14], 71), 0),
        "w_key": draw_w_key(jax.random.fold_in(streams_of[14], 71), 0),
        "w_value": normal_values(streams_of[5], (D, HEADS * DH), D ** -0.5, 0.09375, ((1, 2),)),
        "w_out": normal_values(streams_of[6], (HEADS * DH, D), (HEADS * DH) ** -0.5, 0.125, ((0, 2),)),
        "final_gain": jnp.clip(1.0 + 0.18 * jax.random.normal(streams_of[7], (D,), jnp.float32), 0.1, 1.9),
        "cross_key": draw_cross_key(jax.random.fold_in(streams_of[14], 71), 0),
        "cross_value": normal_values(streams_of[9], (D, HEADS * DH), D ** -0.5, 0.09375, ((1, 2),)),
        "beam_states": draw_beam_states(jax.random.fold_in(streams_of[14], 71), 0),
        "parents": touch_ends(jax.random.randint(streams_of[11], (NQ, BEAMS), 0, BEAMS), jax.random.fold_in(streams_of[11], 1), 0, BEAMS - 1).astype(jnp.int32),
        "dec_gain": jnp.clip(1.0 + 0.18 * jax.random.normal(streams_of[12], (D,), jnp.float32), 0.1, 1.9),
        "dec_query": draw_dec_query(jax.random.fold_in(streams_of[14], 71), 0),
    }


EPS = 1e-06
SCALE = 0.125
NEGATIVE = -1e+30

def rms_scale(entries, gain_vec):
    entries = entries.astype(jnp.float32)
    inverse = lax.rsqrt(lax.optimization_barrier(jnp.mean(entries * entries, axis=-1, keepdims=True)) + EPS)
    return entries * inverse * gain_vec

def reference(tokens, lengths, enc_gain, w_query, w_key, w_value, w_out, final_gain, cross_key, cross_value, beam_states, parents, dec_gain, dec_query):

    def one_question(packed):
        question_tokens, question_lengths, question_states, question_parents = packed
        passages, passage_len, model_width = question_tokens.shape
        flat_rows = question_tokens.reshape(passages * passage_len, model_width)
        normed = rms_scale(flat_rows, enc_gain).astype(jnp.bfloat16)

        def project(matrix):
            return jnp.dot(normed, matrix, preferred_element_type=jnp.float32).astype(jnp.bfloat16).reshape(passages, passage_len, HEADS, DH)
        q_enc = project(w_query)
        k_enc = project(w_key)
        v_enc = project(w_value)
        scores = jnp.einsum('pihd,pjhd->phij', q_enc.astype(jnp.float32), k_enc.astype(jnp.float32)) * SCALE
        live_mask = jnp.arange(passage_len, dtype=jnp.int32)[None, :] < question_lengths[:, None]
        key_mask = live_mask[:, None, None, :]
        peak = lax.optimization_barrier(jnp.max(jnp.where(key_mask, scores, NEGATIVE), axis=-1, keepdims=True))
        expo_terms = jnp.where(key_mask, jnp.exp(scores - peak), 0.0)
        denom = lax.optimization_barrier(jnp.sum(expo_terms, axis=-1, keepdims=True))
        weights_enc = expo_terms.astype(jnp.bfloat16)
        blended = jnp.einsum('phij,pjhd->pihd', weights_enc.astype(jnp.float32), v_enc.astype(jnp.float32))
        blended = blended / jnp.transpose(denom, (0, 2, 1, 3))
        attended = blended.astype(jnp.bfloat16).reshape(passages * passage_len, HEADS * DH)
        encoded = (flat_rows.astype(jnp.float32) + jnp.dot(attended, w_out, preferred_element_type=jnp.float32)).astype(jnp.bfloat16)
        final_rows = rms_scale(encoded, final_gain).astype(jnp.bfloat16)
        ckey = jnp.dot(final_rows, cross_key, preferred_element_type=jnp.float32).astype(jnp.bfloat16).reshape(passages * passage_len, HEADS, DH)
        cval = jnp.dot(final_rows, cross_value, preferred_element_type=jnp.float32).astype(jnp.bfloat16).reshape(passages * passage_len, HEADS, DH)
        chosen = jnp.take(question_states, question_parents, axis=0)
        dec_normed = rms_scale(chosen, dec_gain).astype(jnp.bfloat16)
        dquery = jnp.dot(dec_normed, dec_query, preferred_element_type=jnp.float32).astype(jnp.bfloat16).reshape(BEAMS, HEADS, DH)
        cscore = jnp.einsum('bhd,khd->bhk', dquery.astype(jnp.float32), ckey.astype(jnp.float32)) * SCALE
        slot_mask = live_mask.reshape(passages * passage_len)[None, None, :]
        cpeak = lax.optimization_barrier(jnp.max(jnp.where(slot_mask, cscore, NEGATIVE), axis=-1, keepdims=True))
        cexp = jnp.where(slot_mask, jnp.exp(cscore - cpeak), 0.0)
        ctotal = lax.optimization_barrier(jnp.sum(cexp, axis=-1))
        cweights = cexp.astype(jnp.bfloat16)
        context = jnp.einsum('bhk,khd->bhd', cweights.astype(jnp.float32), cval.astype(jnp.float32)) / ctotal[:, :, None]
        return (encoded.reshape(passages, passage_len, model_width), context.reshape(BEAMS, HEADS * DH))
    encoded_all, context_all = lax.map(one_question, (tokens, lengths, beam_states, parents))
    return (encoded_all, context_all)
```

```python
import jax
import jax.numpy as jnp
from jax import lax
from jax.sharding import PartitionSpec as P

DH = 64


EPS = 1e-06
SCALE = 0.125
NEGATIVE = -1e30


def rms_scale(entries, gain_vec, model_width):
    entries = entries.astype(jnp.float32)
    inverse = lax.rsqrt(jnp.sum(entries * entries, axis=-1, keepdims=True) / model_width + EPS)
    return entries * inverse * gain_vec


def per_device(
    tokens,
    lengths,
    enc_gain,
    w_query,
    w_key,
    w_value,
    w_out,
    final_gain,
    cross_key,
    cross_value,
    beam_states,
    parents,
    dec_gain,
    dec_query,
):
    questions, passages, passage_len, local_cols = tokens.shape
    tp = lax.axis_size("tp")
    pb = lax.axis_size("pb")
    model_width = local_cols * tp
    heads = w_query.shape[1] // DH
    beams = beam_states.shape[1]
    rows = questions * passages * passage_len
    first_slot = lax.axis_index("psg") * passages
    local_lengths = lax.dynamic_slice_in_dim(lengths, first_slot, passages, 1)

    all_states = lax.all_gather(beam_states, "pb", axis=0, tiled=True)
    all_parents = lax.all_gather(parents, "pb", axis=0, tiled=True)
    beam_index = lax.broadcasted_iota(jnp.int32, (pb, beams, beams), 2)
    one_hot = (all_parents[:, :, None] == beam_index).astype(jnp.bfloat16)
    chosen = jnp.einsum("qbc,qcd->qbd", one_hot, all_states, preferred_element_type=jnp.float32)
    dec_normed = rms_scale(chosen, dec_gain, model_width).astype(jnp.bfloat16)
    depth = dec_query.shape[0]
    dec_part = lax.dynamic_slice_in_dim(dec_normed, lax.axis_index("pb") * depth, depth, 2)
    dq_part = jnp.dot(dec_part.reshape(pb * beams, depth), dec_query, preferred_element_type=jnp.float32)
    dquery = lax.psum_scatter(dq_part, "pb", scatter_dimension=0, tiled=True)
    dquery = dquery.astype(jnp.bfloat16).reshape(beams, heads, DH)
    absorbed = jnp.einsum(
        "mhd,bhd->mhb", cross_key.reshape(model_width, heads, DH), dquery, preferred_element_type=jnp.float32
    ).reshape(model_width, heads * beams)
    absorbed = lax.all_to_all(absorbed.astype(jnp.bfloat16), "tp", 0, 1, tiled=True)

    gathered_rows = lax.all_gather(tokens, "tp", axis=3, tiled=True).reshape(rows, model_width)
    normed = rms_scale(gathered_rows, enc_gain, model_width).astype(jnp.bfloat16)

    def project(matrix):
        product = jnp.dot(normed, matrix, preferred_element_type=jnp.float32)
        return product.astype(jnp.bfloat16).reshape(passages, passage_len, heads, DH)

    queries_enc = project(w_query)
    keys_enc = project(w_key)
    values_enc = project(w_value)
    scores = (
        jnp.einsum("nihd,njhd->nhij", queries_enc, keys_enc, preferred_element_type=jnp.float32)
        * SCALE
    )
    slot_index = lax.broadcasted_iota(jnp.int32, (passages, passage_len), 1)
    live = slot_index < local_lengths.reshape(passages, 1)
    key_mask = live[:, None, None, :]
    peak = jnp.max(jnp.where(key_mask, scores, NEGATIVE), axis=-1, keepdims=True)
    expo_terms = jnp.where(key_mask, jnp.exp(scores - peak), 0.0)
    denom = jnp.sum(expo_terms, axis=-1, keepdims=True)
    blended = jnp.einsum(
        "nhij,njhd->nihd",
        expo_terms.astype(jnp.bfloat16),
        values_enc,
        preferred_element_type=jnp.float32,
    )
    blended = blended / jnp.transpose(denom, (0, 2, 1, 3))
    attended = blended.astype(jnp.bfloat16).reshape(rows, heads * DH)
    partial_value = jnp.dot(attended, w_out, preferred_element_type=jnp.float32)
    column_share = lax.psum_scatter(
        partial_value.astype(jnp.bfloat16), "tp", scatter_dimension=1, tiled=True
    ).astype(jnp.float32)
    encoded_local = (
        tokens.reshape(rows, local_cols).astype(jnp.float32) + column_share
    ).astype(jnp.bfloat16)
    encoded_wide = encoded_local.astype(jnp.float32)
    squares = lax.psum(jnp.sum(encoded_wide * encoded_wide, axis=-1), "tp")
    inverse = lax.rsqrt(squares / model_width + EPS)
    gain_part = lax.dynamic_slice_in_dim(
        final_gain, lax.axis_index("tp") * local_cols, local_cols, 0
    )
    final_local = (encoded_wide * inverse[:, None] * gain_part).astype(jnp.bfloat16)
    part_scores = jnp.dot(final_local, absorbed, preferred_element_type=jnp.float32)
    cscores = lax.psum(part_scores, "tp") * SCALE
    live_rows = live.reshape(rows, 1)
    local_peak = jnp.max(jnp.where(live_rows, cscores, NEGATIVE), axis=0)
    cexp = jnp.where(live_rows, jnp.exp(cscores - local_peak), 0.0)
    total = jnp.sum(cexp, axis=0)
    mixed = lax.dot_general(
        cexp.astype(jnp.bfloat16), final_local, (((0,), (0,)), ((), ())), preferred_element_type=jnp.float32
    )
    mixed = lax.all_to_all(mixed.astype(jnp.bfloat16), "tp", 0, 1, tiled=True)
    part = jnp.einsum(
        "hbm,mhd->bhd",
        mixed.reshape(heads, beams, model_width),
        cross_value.reshape(model_width, heads, DH),
        preferred_element_type=jnp.float32,
    )
    mine = lax.axis_index("tp") * heads * beams
    my_peak = lax.dynamic_slice_in_dim(local_peak, mine, heads * beams, 0).reshape(heads, beams).T
    my_total = lax.dynamic_slice_in_dim(total, mine, heads * beams, 0).reshape(heads, beams).T
    whole_peak = lax.pmax(my_peak, "psg")
    factor = jnp.exp(my_peak - whole_peak)
    joined = jnp.concatenate([part * factor[..., None], (my_total * factor)[..., None]], axis=-1)
    joined = lax.psum(joined, "psg")
    context = joined[..., :DH] / joined[..., DH:]
    return (
        encoded_local.reshape(questions, passages, passage_len, local_cols),
        context.reshape(questions, beams, heads * DH),
    )


def solution(mesh):
    in_specs = (
        P("pb", "psg", None, "tp"),
        P("pb", None),
        P(),
        P(None, "tp"),
        P(None, "tp"),
        P(None, "tp"),
        P("tp", None),
        P(),
        P(None, "tp"),
        P(None, "tp"),
        P("pb", None, None),
        P("pb", None),
        P(),
        P("pb", "tp"),
    )
    out_specs = (P("pb", "psg", None, "tp"), P("pb", None, "tp"))
    return jax.shard_map(
        per_device, mesh=mesh, in_specs=in_specs, out_specs=out_specs, check_vma=False
    )
```

```python
import functools

import jax
import jax.numpy as jnp
from jax import lax
from jax.experimental import pallas as pl
from jax.experimental.pallas import tpu as pltpu
from jax.sharding import PartitionSpec as P

DH = 64
EPS = 1e-06
SCALE = 0.125
LOG2E = 1.4426950408889634
NEGATIVE = -1e30
MESH = pl.DeviceIdType.MESH
F32 = jnp.float32
BF16 = jnp.bfloat16


def nt_dot(a, b):
    return lax.dot_general(a, b, (((1,), (1,)), ((), ())), preferred_element_type=F32)


def nn_dot(a, b):
    return jnp.dot(a, b, preferred_element_type=F32)


def lane_fold(x):
    total = x[:, :128]
    for i in range(1, x.shape[1] // 128):
        total = total + x[:, i * 128 : (i + 1) * 128]
    return total


def body(
    sizes,
    tok_hbm, len_ref, eg_ref, wq_hbm, wk_hbm, wv_hbm, wo_hbm, fg_ref, ck_hbm, cv_hbm, beam_ref, par_ref, dg_ref, dec_hbm,
    enc_hbm, ctx_ref,
    tok, xl, xr, wbuf, wo, acc, qkv, att, attp, enc, decw,
    sq, sqp, inv, gq, sc, scp, mix, mixp, bd, dn, dnr, dqp, dqr, stat, stats, ctp, cts,
    lsem, tsend, trecv, psend, precv, ssend, srecv, csend, crecv,
):
    npsg, npb = sizes
    rows, half = tok.shape
    width = 2 * half
    cols = qkv.shape[2]
    heads = cols // DH
    beams = beam_ref.shape[0]
    hb = heads * beams
    plen = 256
    passages = rows // plen
    tp = lax.axis_index("tp")
    psg = lax.axis_index("psg")
    pb = lax.axis_index("pb")
    other = 1 - tp
    mine_f = pl.ds(pl.multiple_of(tp * half, half), half)
    peer_f = pl.ds(pl.multiple_of(other * half, half), half)

    barrier = pltpu.get_barrier_semaphore()
    pl.semaphore_signal(barrier, inc=1, device_id={"tp": other}, device_id_type=MESH)

    def hello_psg(k, c):
        pl.semaphore_signal(barrier, inc=1, device_id={"psg": lax.rem(psg + k, npsg)}, device_id_type=MESH)
        return c

    lax.fori_loop(1, npsg, hello_psg, 0)
    for k in range(1, npb):
        pl.semaphore_signal(barrier, inc=1, device_id={"pb": lax.rem(pb + k, npb)}, device_id_type=MESH)

    copy_tok = pltpu.make_async_copy(tok_hbm, tok, lsem.at[0])
    copy_tok.start()
    w_hbm = (wq_hbm, wk_hbm, wv_hbm)
    copy_w = [[None, None] for _ in range(3)]
    for h, part in enumerate((mine_f, peer_f)):
        for w in range(3):
            copy_w[w][h] = pltpu.make_async_copy(w_hbm[w].at[part, :], wbuf.at[w, h], lsem.at[1 + 2 * w + h])
    copy_dec = pltpu.make_async_copy(dec_hbm, decw, lsem.at[7])
    copy_wo = pltpu.make_async_copy(wo_hbm.at[:, mine_f], wo.at[0], lsem.at[8])
    for w in range(3):
        copy_w[w][0].start()
    copy_dec.start()
    for w in range(3):
        copy_w[w][1].start()
    copy_wo.start()

    chosen = []
    for b in range(beams):
        row = jnp.zeros((1, width), F32)
        for c in range(beams):
            row = row + (par_ref[0, b] == c).astype(F32) * beam_ref[c : c + 1, :].astype(F32)
        chosen.append(row)
    depth = width // npb
    for b in range(beams):
        row = chosen[b]
        ms = jnp.sum(row * row, axis=-1, keepdims=True) * (1.0 / width) + EPS
        row = (row * lax.rsqrt(ms) * dg_ref[...]).astype(BF16).astype(F32)
        for j in range(npb):
            dn[j, b : b + 1, :] = row[:, j * depth : (j + 1) * depth]
    for j in range(npb):
        dn[j, beams:8, :] = jnp.zeros((8 - beams, depth), F32)

    blk = 32
    copy_tok.wait()

    def squares(i, c):
        r = pl.ds(pl.multiple_of(i * blk, blk), blk)
        x = tok[r, :].astype(F32)
        sq[r, :] = lane_fold(x * x)
        return c

    lax.fori_loop(0, rows // blk, squares, 0)

    pl.semaphore_wait(barrier, npsg - 1 + npb - 1 + 1)

    def to_other(src, dst, i):
        return pltpu.make_async_remote_copy(
            src_ref=src, dst_ref=dst, send_sem=tsend.at[i], recv_sem=trecv.at[i],
            device_id={"tp": other}, device_id_type=MESH,
        )

    send_sq = to_other(sq, sqp, 0)
    send_tok = to_other(tok, xr, 1)
    send_wo = to_other(wo_hbm.at[:, peer_f], wo.at[1], 2)
    send_sq.start()
    send_tok.start()

    def to_pb(k, src, dst, base):
        to = lax.rem(pb + k, npb)
        return pltpu.make_async_remote_copy(
            src_ref=src.at[to], dst_ref=dst.at[pb], send_sem=psend.at[base + k - 1], recv_sem=precv.at[base + k - 1],
            device_id={"pb": to}, device_id_type=MESH,
        )

    send_dn = [to_pb(k, dn, dnr, 0) for k in range(1, npb)]
    for s in send_dn:
        s.start()
    dnr[pb] = dn[pb]

    send_sq.wait()

    def normalise_local(i, c):
        r = pl.ds(pl.multiple_of(i * blk, blk), blk)
        ms = jnp.sum(sq[r, :] + sqp[r, :], axis=-1, keepdims=True) * (1.0 / width) + EPS
        v = jnp.broadcast_to(lax.rsqrt(ms), (blk, 128))
        inv[r, :] = v
        x = tok[r, :].astype(F32)
        xl[r, :] = (x * v[:, :1] * eg_ref[:, mine_f]).astype(BF16)
        return c

    lax.fori_loop(0, rows // blk, normalise_local, 0)

    nt = min(512, cols)
    for w in range(3):
        copy_w[w][0].wait()

        def first_half(j, c):
            t = pl.ds(pl.multiple_of(j * nt, nt), nt)
            acc[w, :, t] = nn_dot(xl[...], wbuf[w, 0, :, t])
            return c

        lax.fori_loop(0, cols // nt, first_half, 0)

    copy_ck = [
        pltpu.make_async_copy(ck_hbm.at[mine_f, :], wbuf.at[0, 0], lsem.at[9]),
        pltpu.make_async_copy(ck_hbm.at[peer_f, :], wbuf.at[1, 0], lsem.at[10]),
    ]
    copy_cv = [
        pltpu.make_async_copy(cv_hbm.at[mine_f, :], wbuf.at[2, 0], lsem.at[11]),
        pltpu.make_async_copy(cv_hbm.at[peer_f, :], wbuf.at[0, 1], lsem.at[12]),
    ]
    copy_ck[0].start()
    copy_ck[1].start()
    copy_cv[0].start()

    for s in send_dn:
        s.wait()
    copy_dec.wait()
    dqp[...] = nn_dot(dnr[...].reshape(npb * 8, depth).astype(BF16), decw[...]).reshape(npb, 8, cols)
    send_dq = [to_pb(k, dqp, dqr, npb - 1) for k in range(1, npb)]
    for s in send_dq:
        s.start()
    dqr[pb] = dqp[pb]

    send_tok.wait()
    send_wo.start()

    def normalise_peer(i, c):
        r = pl.ds(pl.multiple_of(i * blk, blk), blk)
        x = xr[r, :].astype(F32)
        xr[r, :] = (x * inv[r, :1] * eg_ref[:, peer_f]).astype(BF16)
        return c

    lax.fori_loop(0, rows // blk, normalise_peer, 0)

    for w in range(3):
        copy_w[w][1].wait()

        def second_half(j, c):
            t = pl.ds(pl.multiple_of(j * nt, nt), nt)
            qkv[w, :, t] = (acc[w, :, t] + nn_dot(xr[...], wbuf[w, 1, :, t])).astype(BF16)
            return c

        lax.fori_loop(0, cols // nt, second_half, 0)
        if w == 0:
            copy_cv[1].start()

    lane = lax.broadcasted_iota(jnp.int32, (plen, 128), 1)
    low = lane < DH
    slot = lax.broadcasted_iota(jnp.int32, (1, plen), 1)
    groups = cols // 256
    send_att = []
    for g in range(groups):
        for p in range(passages):
            key_live = slot < len_ref[0, psg * passages + p]
            r = slice(p * plen, (p + 1) * plen)
            for pair in range(2):
                t = slice(g * 256 + pair * 128, g * 256 + pair * 128 + 128)
                q = qkv[0, r, t]
                zero = jnp.zeros_like(q)
                q2 = jnp.concatenate([jnp.where(low, q, zero), jnp.where(low, zero, q)], axis=0)
                s = jnp.where(key_live, nt_dot(q2, qkv[1, r, t]), NEGATIVE)
                e = jnp.exp2((s - jnp.max(s, axis=-1, keepdims=True)) * (SCALE * LOG2E))
                den = jnp.sum(e, axis=-1, keepdims=True)
                o = nn_dot(e.astype(BF16), qkv[2, r, t]) / den
                att[r, t] = jnp.where(low, o[:plen], o[plen:]).astype(BF16)
        t = slice(g * 256, g * 256 + 256)
        s = to_other(att.at[:, t], attp.at[:, t], 3 + g)
        s.start()
        send_att.append(s)

    for s in send_dq:
        s.wait()
    dq = dqr[0]
    for j in range(1, npb):
        dq = dq + dqr[j]
    dq = dq.astype(BF16).astype(F32)
    head_of = lax.broadcasted_iota(jnp.int32, (heads, cols), 1) // DH
    head_row = lax.broadcasted_iota(jnp.int32, (heads, cols), 0)
    for b in range(beams):
        bd[b * heads : (b + 1) * heads, :] = jnp.where(head_of == head_row, dq[b : b + 1, :], 0.0).astype(BF16)
    mine_h = pl.ds(pl.multiple_of(tp * hb, hb), hb)
    peer_h = pl.ds(pl.multiple_of(other * hb, hb), hb)
    kt = min(512, half)

    for f in range(2):
        copy_ck[f].wait()

        def absorb(j, c):
            t = pl.ds(pl.multiple_of(j * kt, kt), kt)
            start = (tp if f == 0 else other) * half + j * kt
            a = nt_dot(bd[...], wbuf[f, 0, t, :]) * fg_ref[:, pl.ds(pl.multiple_of(start, kt), kt)]
            if f == 0:
                gq[mine_h, t] = a.astype(BF16)
            else:
                mix[mine_h, t] = a.astype(BF16)
            return c

        lax.fori_loop(0, half // kt, absorb, 0)
    send_gq = to_other(mix.at[mine_h, :], gq.at[mine_h, :], 3 + groups)
    send_gq.start()

    copy_wo.wait()

    def out_own(j, c):
        t = pl.ds(pl.multiple_of(j * nt, nt), nt)
        per = cols // nt
        acc[j // per, :, pl.ds(pl.multiple_of((j % per) * nt, nt), nt)] = nn_dot(att[...], wo[0, :, t])
        return c

    lax.fori_loop(0, half // nt, out_own, 0)
    for s in send_att:
        s.wait()
    send_gq.wait()
    send_wo.wait()
    sq[...] = jnp.zeros_like(sq)
    sc[...] = jnp.zeros_like(sc)

    def out_peer(j, c):
        t = pl.ds(pl.multiple_of(j * nt, nt), nt)
        per = cols // nt
        a = acc[j // per, :, pl.ds(pl.multiple_of((j % per) * nt, nt), nt)]
        e = (tok[:, t].astype(F32) + (a + nn_dot(attp[...], wo[1, :, t]))).astype(BF16)
        enc[:, t] = e
        wide = e.astype(F32)
        sq[...] += lane_fold(wide * wide)
        sc[...] += nt_dot(e, gq[:, t])
        return c

    lax.fori_loop(0, half // nt, out_peer, 0)
    copy_enc = pltpu.make_async_copy(enc, enc_hbm, lsem.at[13])
    send_sq2 = to_other(sq, sqp, 0)
    send_sc = to_other(sc, scp, 4 + groups)
    send_sq2.start()
    send_sc.start()
    copy_enc.start()
    send_sq2.wait()
    send_sc.wait()

    x = jnp.sum(sq[...] + sqp[...], axis=-1, keepdims=True) * (1.0 / width) + EPS
    iv = lax.rsqrt(x)
    s = (sc[...] + scp[...]) * iv * SCALE
    row = lax.broadcasted_iota(jnp.int32, (rows, 1), 0)
    limit = jnp.zeros((rows, 1), jnp.int32) + len_ref[0, psg * passages]
    for p in range(1, passages):
        limit = jnp.where(row >= p * plen, p * plen + len_ref[0, psg * passages + p], limit)
    live = row < limit
    s = jnp.where(live, s, NEGATIVE)
    peak = jnp.max(s, axis=0, keepdims=True)
    e = jnp.where(live, jnp.exp2((s - peak) * LOG2E), 0.0)
    wi = (e * iv).astype(BF16).astype(F32)
    total = jnp.sum(wi * (x * iv), axis=0, keepdims=True)
    wt = jnp.transpose(wi).astype(BF16)
    stat[0:1, :] = peak
    stat[1:2, :] = total
    stat[2:8, :] = jnp.zeros((6, 128), F32)

    def to_psg(k, src, dst, ss, rs):
        return pltpu.make_async_remote_copy(
            src_ref=src, dst_ref=dst.at[psg], send_sem=ss.at[k - 1], recv_sem=rs.at[k - 1],
            device_id={"psg": lax.rem(psg + k, npsg)}, device_id_type=MESH,
        )

    def start_stat(k, c):
        to_psg(k, stat, stats, ssend, srecv).start()
        return c

    lax.fori_loop(1, npsg, start_stat, 0)
    stats[psg] = stat[...]

    def mixed(j, c):
        t = pl.ds(pl.multiple_of(j * nt, nt), nt)
        gain = fg_ref[:, pl.ds(pl.multiple_of(tp * half + j * nt, nt), nt)]
        mix[:, t] = (nn_dot(wt, enc[:, t]) * gain).astype(BF16)
        return c

    lax.fori_loop(0, half // nt, mixed, 0)
    send_mix = to_other(mix.at[peer_h, :], mixp, 5 + groups)
    send_mix.start()

    def wait_stat(k, c):
        to_psg(k, stat, stats, ssend, srecv).wait()
        return c

    lax.fori_loop(1, npsg, wait_stat, 0)
    peaks = jnp.max(stats[:, 0:1, :], axis=0)
    totals = jnp.sum(stats[:, 1:2, :] * jnp.exp2((stats[:, 0:1, :] - peaks) * LOG2E), axis=0)
    factor = jnp.exp2((peak - peaks) * LOG2E) / totals
    sq[0:128, :] = jnp.transpose(jnp.broadcast_to(factor, (128, 128)))
    scale_col = sq[mine_h, :][:, :1]

    ct = 256
    r_head = lax.rem(lax.broadcasted_iota(jnp.int32, (hb, ct), 0), heads)
    c_head = lax.broadcasted_iota(jnp.int32, (hb, ct), 1) // DH

    copy_cv[0].wait()
    for g in range(cols // ct):
        t = slice(g * ct, (g + 1) * ct)
        acc[0, 0:hb, t] = nn_dot(mix[mine_h, :], wbuf[2, 0, :, t])
    copy_cv[1].wait()
    send_mix.wait()
    for g in range(cols // ct):
        t = slice(g * ct, (g + 1) * ct)
        m = (acc[0, 0:hb, t] + nn_dot(mixp[...], wbuf[0, 1, :, t])) * scale_col
        m = jnp.where(r_head == c_head + g * (ct // DH), m, 0.0)
        for b in range(beams):
            ctp[b : b + 1, t] = jnp.sum(m[b * heads : (b + 1) * heads], axis=0, keepdims=True)

    def start_ctx(k, c):
        to_psg(k, ctp, cts, csend, crecv).start()
        return c

    lax.fori_loop(1, npsg, start_ctx, 0)
    cts[psg] = ctp[...]

    def wait_ctx(k, c):
        to_psg(k, ctp, cts, csend, crecv).wait()
        return c

    lax.fori_loop(1, npsg, wait_ctx, 0)
    ctx_ref[...] = jnp.sum(cts[...], axis=0)
    copy_enc.wait()


def per_device(
    tokens, lengths, enc_gain, w_query, w_key, w_value, w_out, final_gain, cross_key, cross_value,
    beam_states, parents, dec_gain, dec_query,
):
    questions, passages, plen, half = tokens.shape
    rows = questions * passages * plen
    cols = w_query.shape[1]
    heads = cols // DH
    beams = beam_states.shape[1]
    hb = heads * beams
    width = 2 * half
    npsg, npb = lax.axis_size("psg"), lax.axis_size("pb")
    groups = cols // 256
    vmem = pl.BlockSpec(memory_space=pltpu.VMEM)
    smem = pl.BlockSpec(memory_space=pltpu.SMEM)
    hbm = pl.BlockSpec(memory_space=pl.ANY)
    V, D = pltpu.VMEM, pltpu.SemaphoreType.DMA
    encoded, context = pl.pallas_call(
        functools.partial(body, (npsg, npb)),
        out_shape=(
            jax.ShapeDtypeStruct((rows, half), BF16),
            jax.ShapeDtypeStruct((beams, cols), F32),
        ),
        in_specs=[hbm, smem, vmem, hbm, hbm, hbm, hbm, vmem, hbm, hbm, vmem, smem, vmem, hbm],
        out_specs=(hbm, vmem),
        scratch_shapes=[
            V((rows, half), BF16),
            V((rows, half), BF16),
            V((rows, half), BF16),
            V((3, 2, half, cols), BF16),
            V((2, cols, half), BF16),
            V((3, rows, cols), F32),
            V((3, rows, cols), BF16),
            V((rows, cols), BF16),
            V((rows, cols), BF16),
            V((rows, half), BF16),
            V((width // npb, cols), BF16),
            V((rows, 128), F32),
            V((rows, 128), F32),
            V((rows, 128), F32),
            V((2 * hb, half), BF16),
            V((rows, 2 * hb), F32),
            V((rows, 2 * hb), F32),
            V((2 * hb, half), BF16),
            V((hb, half), BF16),
            V((hb, cols), BF16),
            V((npb, 8, width // npb), F32),
            V((npb, 8, width // npb), F32),
            V((npb, 8, cols), F32),
            V((npb, 8, cols), F32),
            V((8, 2 * hb), F32),
            V((npsg, 8, 2 * hb), F32),
            V((beams, cols), F32),
            V((npsg, beams, cols), F32),
            D((14,)),
            D((6 + groups,)),
            D((6 + groups,)),
            D((2 * (npb - 1),)),
            D((2 * (npb - 1),)),
            D((npsg - 1,)),
            D((npsg - 1,)),
            D((npsg - 1,)),
            D((npsg - 1,)),
        ],
        compiler_params=pltpu.CompilerParams(
            collective_id=0, has_side_effects=True, vmem_limit_bytes=60 * 2**20
        ),
    )(
        tokens.reshape(rows, half), lengths, enc_gain.reshape(1, width), w_query, w_key, w_value, w_out,
        final_gain.reshape(1, width), cross_key, cross_value, beam_states.reshape(beams, width), parents,
        dec_gain.reshape(1, width), dec_query,
    )
    return (
        encoded.reshape(questions, passages, plen, half),
        context.reshape(questions, beams, cols),
    )


def solution(mesh):
    in_specs = (
        P("pb", "psg", None, "tp"),
        P("pb", None),
        P(),
        P(None, "tp"),
        P(None, "tp"),
        P(None, "tp"),
        P("tp", None),
        P(),
        P(None, "tp"),
        P(None, "tp"),
        P("pb", None, None),
        P("pb", None),
        P(),
        P("pb", "tp"),
    )
    out_specs = (P("pb", "psg", None, "tp"), P("pb", None, "tp"))
    return jax.shard_map(
        per_device, mesh=mesh, in_specs=in_specs, out_specs=out_specs, check_vma=False
    )
```

```python
import functools

import jax
import jax.numpy as jnp
from jax import lax
from jax.experimental import pallas as pl
from jax.experimental.pallas import tpu as pltpu
from jax.sharding import PartitionSpec as P

DH = 64
EPS = 1e-06
SCALE = 0.125
LOG2E = 1.4426950408889634
NEGATIVE = -1e30
MESH = pl.DeviceIdType.MESH
F32 = jnp.float32
BF16 = jnp.bfloat16


def nt_dot(a, b):
    return lax.dot_general(a, b, (((1,), (1,)), ((), ())), preferred_element_type=F32)


def nn_dot(a, b):
    return jnp.dot(a, b, preferred_element_type=F32)


def lane_fold(x):
    total = x[:, :128]
    for i in range(1, x.shape[1] // 128):
        total = total + x[:, i * 128 : (i + 1) * 128]
    return total


def body(
    sizes,
    tok_hbm, len_ref, eg_ref, wq_hbm, wk_hbm, wv_hbm, wo_hbm, fg_ref, ck_hbm, cv_hbm, beam_ref, par_ref, dg_ref, dec_hbm,
    enc_hbm, ctx_ref,
    tok, xl, xr, wbuf, wo, acc, qkv, att, attp, enc, decw,
    sq, sqp, inv, gq, sc, scp, mix, mixp, bd, dn, dnr, dqp, dqr, stat, stats, ctp, cts,
    lsem, tsend, trecv, psend, precv, ssend, srecv, csend, crecv,
):
    npsg, npb = sizes
    rows, half = tok.shape
    width = 2 * half
    cols = qkv.shape[2]
    heads = cols // DH
    beams = beam_ref.shape[0]
    hb = heads * beams
    plen = 256
    passages = rows // plen
    tp = lax.axis_index("tp")
    psg = lax.axis_index("psg")
    pb = lax.axis_index("pb")
    other = 1 - tp
    mine_f = pl.ds(pl.multiple_of(tp * half, half), half)
    peer_f = pl.ds(pl.multiple_of(other * half, half), half)

    barrier = pltpu.get_barrier_semaphore()
    pl.semaphore_signal(barrier, inc=1, device_id={"tp": other}, device_id_type=MESH)

    def hello_psg(k, c):
        pl.semaphore_signal(barrier, inc=1, device_id={"psg": lax.rem(psg + k, npsg)}, device_id_type=MESH)
        return c

    lax.fori_loop(1, npsg, hello_psg, 0)
    for k in range(1, npb):
        pl.semaphore_signal(barrier, inc=1, device_id={"pb": lax.rem(pb + k, npb)}, device_id_type=MESH)

    copy_tok = pltpu.make_async_copy(tok_hbm, tok, lsem.at[0])
    copy_tok.start()
    w_hbm = (wq_hbm, wk_hbm, wv_hbm)
    copy_w = [[None, None] for _ in range(3)]
    for h, part in enumerate((mine_f, peer_f)):
        for w in range(3):
            copy_w[w][h] = pltpu.make_async_copy(w_hbm[w].at[part, :], wbuf.at[w, h], lsem.at[1 + 2 * w + h])
    copy_dec = pltpu.make_async_copy(dec_hbm, decw, lsem.at[7])
    copy_wo = pltpu.make_async_copy(wo_hbm.at[:, mine_f], wo.at[0], lsem.at[8])
    for w in range(3):
        copy_w[w][0].start()
    copy_dec.start()
    for w in range(3):
        copy_w[w][1].start()
    copy_wo.start()

    chosen = []
    for b in range(beams):
        row = jnp.zeros((1, width), F32)
        for c in range(beams):
            row = row + (par_ref[0, b] == c).astype(F32) * beam_ref[c : c + 1, :].astype(F32)
        chosen.append(row)
    depth = width // npb
    for b in range(beams):
        row = chosen[b]
        ms = jnp.sum(row * row, axis=-1, keepdims=True) * (1.0 / width) + EPS
        row = (row * lax.rsqrt(ms) * dg_ref[...]).astype(BF16).astype(F32)
        for j in range(npb):
            dn[j, b : b + 1, :] = row[:, j * depth : (j + 1) * depth]
    for j in range(npb):
        dn[j, beams:8, :] = jnp.zeros((8 - beams, depth), F32)

    blk = 32
    copy_tok.wait()

    def scale_local(i, c):
        r = pl.ds(pl.multiple_of(i * blk, blk), blk)
        x = tok[r, :].astype(F32)
        sq[r, :] = lane_fold(x * x)
        xl[r, :] = (x * eg_ref[:, mine_f]).astype(BF16)
        return c

    lax.fori_loop(0, rows // blk, scale_local, 0)

    pl.semaphore_wait(barrier, npsg - 1 + npb - 1 + 1)

    def to_other(src, dst, i):
        return pltpu.make_async_remote_copy(
            src_ref=src, dst_ref=dst, send_sem=tsend.at[i], recv_sem=trecv.at[i],
            device_id={"tp": other}, device_id_type=MESH,
        )

    send_sq = to_other(sq, sqp, 0)
    send_tok = to_other(xl, xr, 1)
    send_wo = to_other(wo_hbm.at[:, peer_f], wo.at[1], 2)
    send_tok.start()
    send_sq.start()

    def to_pb(k, src, dst, base):
        to = lax.rem(pb + k, npb)
        return pltpu.make_async_remote_copy(
            src_ref=src.at[to], dst_ref=dst.at[pb], send_sem=psend.at[base + k - 1], recv_sem=precv.at[base + k - 1],
            device_id={"pb": to}, device_id_type=MESH,
        )

    send_dn = [to_pb(k, dn, dnr, 0) for k in range(1, npb)]
    for s in send_dn:
        s.start()
    dnr[pb] = dn[pb]

    nt = min(512, cols)
    for w in range(3):
        copy_w[w][0].wait()

        def first_half(j, c):
            t = pl.ds(pl.multiple_of(j * nt, nt), nt)
            acc[w, :, t] = nn_dot(xl[...], wbuf[w, 0, :, t])
            return c

        lax.fori_loop(0, cols // nt, first_half, 0)

    copy_ck = [
        pltpu.make_async_copy(ck_hbm.at[mine_f, :], wbuf.at[0, 0], lsem.at[9]),
        pltpu.make_async_copy(ck_hbm.at[peer_f, :], wbuf.at[1, 0], lsem.at[10]),
    ]
    copy_cv = [
        pltpu.make_async_copy(cv_hbm.at[mine_f, :], wbuf.at[2, 0], lsem.at[11]),
        pltpu.make_async_copy(cv_hbm.at[peer_f, :], wbuf.at[0, 1], lsem.at[12]),
    ]
    copy_ck[0].start()
    copy_ck[1].start()
    copy_cv[0].start()

    for s in send_dn:
        s.wait()
    copy_dec.wait()
    dqp[...] = nn_dot(dnr[...].reshape(npb * 8, depth).astype(BF16), decw[...]).reshape(npb, 8, cols)
    send_dq = [to_pb(k, dqp, dqr, npb - 1) for k in range(1, npb)]
    for s in send_dq:
        s.start()
    dqr[pb] = dqp[pb]

    send_tok.wait()
    send_wo.start()
    send_sq.wait()

    def inverse(i, c):
        r = pl.ds(pl.multiple_of(i * blk, blk), blk)
        ms = jnp.sum(sq[r, :] + sqp[r, :], axis=-1, keepdims=True) * (1.0 / width) + EPS
        inv[r, :] = jnp.broadcast_to(lax.rsqrt(ms), (blk, 128))
        return c

    lax.fori_loop(0, rows // blk, inverse, 0)

    for w in range(3):
        copy_w[w][1].wait()

        def second_half(j, c):
            t = pl.ds(pl.multiple_of(j * nt, nt), nt)
            scale = jnp.concatenate([inv[...]] * (nt // 128), axis=1)
            qkv[w, :, t] = ((acc[w, :, t] + nn_dot(xr[...], wbuf[w, 1, :, t])) * scale).astype(BF16)
            return c

        lax.fori_loop(0, cols // nt, second_half, 0)
        if w == 0:
            copy_cv[1].start()

    lane = lax.broadcasted_iota(jnp.int32, (plen, 128), 1)
    low = lane < DH
    slot = lax.broadcasted_iota(jnp.int32, (1, plen), 1)
    groups = cols // 256
    send_att = []
    for g in range(groups):
        for p in range(passages):
            key_live = slot < len_ref[0, psg * passages + p]
            r = slice(p * plen, (p + 1) * plen)
            for pair in range(2):
                t = slice(g * 256 + pair * 128, g * 256 + pair * 128 + 128)
                q = qkv[0, r, t]
                zero = jnp.zeros_like(q)
                q2 = jnp.concatenate([jnp.where(low, q, zero), jnp.where(low, zero, q)], axis=0)
                s = jnp.where(key_live, nt_dot(q2, qkv[1, r, t]), NEGATIVE)
                e = jnp.exp2((s - jnp.max(s, axis=-1, keepdims=True)) * (SCALE * LOG2E))
                den = jnp.sum(e, axis=-1, keepdims=True)
                o = nn_dot(e.astype(BF16), qkv[2, r, t]) / den
                att[r, t] = jnp.where(low, o[:plen], o[plen:]).astype(BF16)
        t = slice(g * 256, g * 256 + 256)
        s = to_other(att.at[:, t], attp.at[:, t], 3 + g)
        s.start()
        send_att.append(s)

    for s in send_dq:
        s.wait()
    dq = dqr[0]
    for j in range(1, npb):
        dq = dq + dqr[j]
    dq = dq.astype(BF16).astype(F32)
    head_of = lax.broadcasted_iota(jnp.int32, (heads, cols), 1) // DH
    head_row = lax.broadcasted_iota(jnp.int32, (heads, cols), 0)
    for b in range(beams):
        bd[b * heads : (b + 1) * heads, :] = jnp.where(head_of == head_row, dq[b : b + 1, :], 0.0).astype(BF16)
    mine_h = pl.ds(pl.multiple_of(tp * hb, hb), hb)
    peer_h = pl.ds(pl.multiple_of(other * hb, hb), hb)
    kt = min(512, half)

    for f in range(2):
        copy_ck[f].wait()

        def absorb(j, c):
            t = pl.ds(pl.multiple_of(j * kt, kt), kt)
            start = (tp if f == 0 else other) * half + j * kt
            a = nt_dot(bd[...], wbuf[f, 0, t, :]) * fg_ref[:, pl.ds(pl.multiple_of(start, kt), kt)]
            if f == 0:
                gq[mine_h, t] = a.astype(BF16)
            else:
                mix[mine_h, t] = a.astype(BF16)
            return c

        lax.fori_loop(0, half // kt, absorb, 0)
    send_gq = to_other(mix.at[mine_h, :], gq.at[mine_h, :], 3 + groups)
    send_gq.start()

    copy_wo.wait()

    def out_own(j, c):
        t = pl.ds(pl.multiple_of(j * nt, nt), nt)
        per = cols // nt
        acc[j // per, :, pl.ds(pl.multiple_of((j % per) * nt, nt), nt)] = nn_dot(att[...], wo[0, :, t])
        return c

    lax.fori_loop(0, half // nt, out_own, 0)
    for s in send_att:
        s.wait()
    send_gq.wait()
    send_wo.wait()
    sq[...] = jnp.zeros_like(sq)
    sc[0 : 2 * hb, :] = jnp.zeros((2 * hb, rows), F32)

    def out_peer(j, c):
        t = pl.ds(pl.multiple_of(j * nt, nt), nt)
        per = cols // nt
        a = acc[j // per, :, pl.ds(pl.multiple_of((j % per) * nt, nt), nt)]
        e = (tok[:, t].astype(F32) + (a + nn_dot(attp[...], wo[1, :, t]))).astype(BF16)
        enc[:, t] = e
        wide = e.astype(F32)
        sq[...] += lane_fold(wide * wide)
        sc[0 : 2 * hb, :] += nt_dot(gq[:, t], e)
        return c

    lax.fori_loop(0, half // nt, out_peer, 0)
    copy_enc = pltpu.make_async_copy(enc, enc_hbm, lsem.at[13])
    sc[2 * hb : 2 * hb + 8, :] = jnp.broadcast_to(jnp.sum(jnp.transpose(sq[...]), axis=0, keepdims=True), (8, rows))
    send_sc = to_other(sc, scp, 4 + groups)
    send_sc.start()
    copy_enc.start()
    send_sc.wait()

    both = sc[...] + scp[...]
    x = both[2 * hb : 2 * hb + 1, :] * (1.0 / width) + EPS
    iv = lax.rsqrt(x)
    at = lax.broadcasted_iota(jnp.int32, (1, rows), 1)
    limit = jnp.zeros((1, rows), jnp.int32) + len_ref[0, psg * passages]
    for p in range(1, passages):
        limit = jnp.where(at >= p * plen, p * plen + len_ref[0, psg * passages + p], limit)
    live = at < limit
    s = jnp.where(live, both[0 : 2 * hb, :] * (iv * SCALE), NEGATIVE)
    peak = jnp.max(s, axis=1, keepdims=True)
    e = jnp.where(live, jnp.exp2((s - peak) * LOG2E), 0.0)
    wt = (e * iv).astype(BF16)
    total = jnp.sum(wt.astype(F32) * (x * iv), axis=1, keepdims=True)

    def to_psg(k, src, dst, ss, rs):
        return pltpu.make_async_remote_copy(
            src_ref=src, dst_ref=dst.at[psg], send_sem=ss.at[k - 1], recv_sem=rs.at[k - 1],
            device_id={"psg": lax.rem(psg + k, npsg)}, device_id_type=MESH,
        )

    def mixed(j, c):
        t = pl.ds(pl.multiple_of(j * nt, nt), nt)
        gain = fg_ref[:, pl.ds(pl.multiple_of(tp * half + j * nt, nt), nt)]
        mix[:, t] = (nn_dot(wt, enc[:, t]) * gain).astype(BF16)
        return c

    lax.fori_loop(0, half // nt, mixed, 0)
    send_mix = to_other(mix.at[peer_h, :], mixp, 5 + groups)
    send_mix.start()
    first = lax.broadcasted_iota(jnp.int32, (2 * hb, 128), 1) == 0
    stat[...] = jnp.transpose(jnp.where(first, peak, total))[0:8, :]

    def start_stat(k, c):
        to_psg(k, stat, stats, ssend, srecv).start()
        return c

    lax.fori_loop(1, npsg, start_stat, 0)
    stats[psg] = stat[...]


    ct = 256
    r_head = lax.rem(lax.broadcasted_iota(jnp.int32, (hb, ct), 0), heads)
    c_head = lax.broadcasted_iota(jnp.int32, (hb, ct), 1) // DH

    copy_cv[0].wait()
    for g in range(cols // ct):
        t = slice(g * ct, (g + 1) * ct)
        acc[0, 0:hb, t] = nn_dot(mix[mine_h, :], wbuf[2, 0, :, t])
    def wait_stat(k, c):
        to_psg(k, stat, stats, ssend, srecv).wait()
        return c

    lax.fori_loop(1, npsg, wait_stat, 0)
    peaks = jnp.max(stats[:, 0:1, :], axis=0)
    totals = jnp.sum(stats[:, 1:2, :] * jnp.exp2((stats[:, 0:1, :] - peaks) * LOG2E), axis=0)
    factor = jnp.exp2((stat[0:1, :] - peaks) * LOG2E) / totals
    sq[0:128, :] = jnp.transpose(jnp.broadcast_to(factor, (128, 128)))
    scale_col = sq[mine_h, :][:, :1]

    copy_cv[1].wait()
    send_mix.wait()
    for g in range(cols // ct):
        t = slice(g * ct, (g + 1) * ct)
        m = (acc[0, 0:hb, t] + nn_dot(mixp[...], wbuf[0, 1, :, t])) * scale_col
        m = jnp.where(r_head == c_head + g * (ct // DH), m, 0.0)
        for b in range(beams):
            ctp[b : b + 1, t] = jnp.sum(m[b * heads : (b + 1) * heads], axis=0, keepdims=True)

    def start_ctx(k, c):
        to_psg(k, ctp, cts, csend, crecv).start()
        return c

    lax.fori_loop(1, npsg, start_ctx, 0)
    cts[psg] = ctp[...]

    def wait_ctx(k, c):
        to_psg(k, ctp, cts, csend, crecv).wait()
        return c

    lax.fori_loop(1, npsg, wait_ctx, 0)
    ctx_ref[...] = jnp.sum(cts[...], axis=0)
    copy_enc.wait()


def writer(enc_hbm, ctx_hbm, enc_out, ctx_out, sem):
    n = sem.shape[0] - 1
    rows = enc_hbm.shape[0] // n
    copies = [
        pltpu.make_async_copy(enc_hbm.at[pl.ds(i * rows, rows), :], enc_out.at[pl.ds(i * rows, rows), :], sem.at[i])
        for i in range(n)
    ]
    copies.append(pltpu.make_async_copy(ctx_hbm, ctx_out, sem.at[n]))
    for c in copies:
        c.start()
    for c in copies:
        c.wait()


def per_device(
    tokens, lengths, enc_gain, w_query, w_key, w_value, w_out, final_gain, cross_key, cross_value,
    beam_states, parents, dec_gain, dec_query,
):
    questions, passages, plen, half = tokens.shape
    rows = questions * passages * plen
    cols = w_query.shape[1]
    heads = cols // DH
    beams = beam_states.shape[1]
    hb = heads * beams
    width = 2 * half
    npsg, npb = lax.axis_size("psg"), lax.axis_size("pb")
    groups = cols // 256
    vmem = pl.BlockSpec(memory_space=pltpu.VMEM)
    smem = pl.BlockSpec(memory_space=pltpu.SMEM)
    hbm = pl.BlockSpec(memory_space=pl.ANY)
    V, D = pltpu.VMEM, pltpu.SemaphoreType.DMA
    encoded, context = pl.pallas_call(
        functools.partial(body, (npsg, npb)),
        out_shape=(
            jax.ShapeDtypeStruct((rows, half), BF16),
            jax.ShapeDtypeStruct((beams, cols), F32),
        ),
        in_specs=[hbm, smem, vmem, hbm, hbm, hbm, hbm, vmem, hbm, hbm, vmem, smem, vmem, hbm],
        out_specs=(hbm, vmem),
        scratch_shapes=[
            V((rows, half), BF16),
            V((rows, half), BF16),
            V((rows, half), BF16),
            V((3, 2, half, cols), BF16),
            V((2, cols, half), BF16),
            V((3, rows, cols), F32),
            V((3, rows, cols), BF16),
            V((rows, cols), BF16),
            V((rows, cols), BF16),
            V((rows, half), BF16),
            V((width // npb, cols), BF16),
            V((rows, 128), F32),
            V((rows, 128), F32),
            V((rows, 128), F32),
            V((2 * hb, half), BF16),
            V((2 * hb + 8, rows), F32),
            V((2 * hb + 8, rows), F32),
            V((2 * hb, half), BF16),
            V((hb, half), BF16),
            V((hb, cols), BF16),
            V((npb, 8, width // npb), F32),
            V((npb, 8, width // npb), F32),
            V((npb, 8, cols), F32),
            V((npb, 8, cols), F32),
            V((8, 2 * hb), F32),
            V((npsg, 8, 2 * hb), F32),
            V((beams, cols), F32),
            V((npsg, beams, cols), F32),
            D((14,)),
            D((6 + groups,)),
            D((6 + groups,)),
            D((2 * (npb - 1),)),
            D((2 * (npb - 1),)),
            D((npsg - 1,)),
            D((npsg - 1,)),
            D((npsg - 1,)),
            D((npsg - 1,)),
        ],
        compiler_params=pltpu.CompilerParams(
            collective_id=0, has_side_effects=True, vmem_limit_bytes=60 * 2**20
        ),
    )(
        tokens.reshape(rows, half), lengths, enc_gain.reshape(1, width), w_query, w_key, w_value, w_out,
        final_gain.reshape(1, width), cross_key, cross_value, beam_states.reshape(beams, width), parents,
        dec_gain.reshape(1, width), dec_query,
    )
    encoded, context = pl.pallas_call(
        writer,
        out_shape=(
            jax.ShapeDtypeStruct((rows, half), BF16),
            jax.ShapeDtypeStruct((beams, cols), F32),
        ),
        in_specs=[hbm, hbm],
        out_specs=(hbm, hbm),
        scratch_shapes=[D((9,))],
    )(encoded, context)
    return (
        encoded.reshape(questions, passages, plen, half),
        context.reshape(questions, beams, cols),
    )


def solution(mesh):
    in_specs = (
        P("pb", "psg", None, "tp"),
        P("pb", None),
        P(),
        P(None, "tp"),
        P(None, "tp"),
        P(None, "tp"),
        P("tp", None),
        P(),
        P(None, "tp"),
        P(None, "tp"),
        P("pb", None, None),
        P("pb", None),
        P(),
        P("pb", "tp"),
    )
    out_specs = (P("pb", "psg", None, "tp"), P("pb", None, "tp"))
    return jax.shard_map(
        per_device, mesh=mesh, in_specs=in_specs, out_specs=out_specs, check_vma=False
    )
```

```python
import functools

import jax
import jax.numpy as jnp
from jax import lax
from jax.experimental import pallas as pl
from jax.experimental.pallas import tpu as pltpu
from jax.sharding import PartitionSpec as P

DH = 64
EPS = 1e-06
SCALE = 0.125
LOG2E = 1.4426950408889634
NEGATIVE = -1e30
MESH = pl.DeviceIdType.MESH
F32 = jnp.float32
BF16 = jnp.bfloat16


def nt_dot(a, b):
    return lax.dot_general(a, b, (((1,), (1,)), ((), ())), preferred_element_type=F32)


def nn_dot(a, b):
    return jnp.dot(a, b, preferred_element_type=F32)


def lane_fold(x):
    total = x[:, :128]
    for i in range(1, x.shape[1] // 128):
        total = total + x[:, i * 128 : (i + 1) * 128]
    return total


def body(
    sizes,
    tok_hbm, len_ref, eg_ref, wq_hbm, wk_hbm, wv_hbm, wo_hbm, fg_ref, ck_hbm, cv_hbm, beam_ref, par_ref, dg_ref, dec_hbm,
    enc_hbm, ctx_ref,
    tok, xl, xr, wbuf, wo, acc, qkv, att, attp, enc, decw,
    sq, sqp, inv, gq, sc, scp, mix, mixp, bd, dn, dnr, dqp, dqr, stat, stats, ctf, ctp, cts, xs, ckb, gpart, gqa, gqp,
    lsem, tsend, trecv, psend, precv, ssend, srecv, csend, crecv, gsend, grecv,
):
    npsg, npb = sizes
    rows, half = tok.shape
    width = 2 * half
    cols = qkv.shape[2]
    heads = cols // DH
    beams = beam_ref.shape[0]
    hb = heads * beams
    plen = 256
    passages = rows // plen
    tp = lax.axis_index("tp")
    psg = lax.axis_index("psg")
    pb = lax.axis_index("pb")
    other = 1 - tp
    mine_f = pl.ds(pl.multiple_of(tp * half, half), half)
    peer_f = pl.ds(pl.multiple_of(other * half, half), half)

    barrier = pltpu.get_barrier_semaphore()
    pl.semaphore_signal(barrier, inc=1, device_id={"tp": other}, device_id_type=MESH)

    def hello_psg(k, c):
        pl.semaphore_signal(barrier, inc=1, device_id={"psg": lax.rem(psg + k, npsg)}, device_id_type=MESH)
        return c

    lax.fori_loop(1, npsg, hello_psg, 0)
    for k in range(1, npb):
        pl.semaphore_signal(barrier, inc=1, device_id={"pb": lax.rem(pb + k, npb)}, device_id_type=MESH)

    parts = 4
    prow = rows // parts
    copy_tok = [
        pltpu.make_async_copy(tok_hbm.at[pl.ds(i * prow, prow), :], tok.at[pl.ds(i * prow, prow), :], lsem.at[10 + i])
        for i in range(parts)
    ]
    for c in copy_tok:
        c.start()
    w_hbm = (wq_hbm, wk_hbm, wv_hbm)
    copy_w = [[None, None] for _ in range(3)]
    for h, part in enumerate((mine_f, peer_f)):
        for w in range(3):
            copy_w[w][h] = pltpu.make_async_copy(w_hbm[w].at[part, :], wbuf.at[w, h], lsem.at[1 + 2 * w + h])
    copy_dec = pltpu.make_async_copy(dec_hbm, decw, lsem.at[7])
    copy_wo = pltpu.make_async_copy(wo_hbm.at[:, mine_f], wo.at[0], lsem.at[8])
    for w in range(3):
        copy_w[w][0].start()
    copy_dec.start()
    fc = half // npsg
    copy_ck = [
        pltpu.make_async_copy(ck_hbm.at[pl.ds(pl.multiple_of(c * half + psg * fc, fc), fc), :], ckb.at[f], lsem.at[14 + f])
        for f, c in enumerate((tp, other))
    ]
    for c in copy_ck:
        c.start()
    for w in range(3):
        copy_w[w][1].start()
    copy_wo.start()

    chosen = []
    for b in range(beams):
        row = jnp.zeros((1, width), F32)
        for c in range(beams):
            row = row + (par_ref[0, b] == c).astype(F32) * beam_ref[c : c + 1, :].astype(F32)
        chosen.append(row)
    depth = width // npb
    for b in range(beams):
        row = chosen[b]
        ms = jnp.sum(row * row, axis=-1, keepdims=True) * (1.0 / width) + EPS
        row = (row * lax.rsqrt(ms) * dg_ref[...]).astype(BF16).astype(F32)
        for j in range(npb):
            dn[j, b : b + 1, :] = row[:, j * depth : (j + 1) * depth]
    for j in range(npb):
        dn[j, beams:8, :] = jnp.zeros((8 - beams, depth), F32)

    blk = 32

    def scale_local(i, c):
        r = pl.ds(pl.multiple_of(i * blk, blk), blk)
        x = tok[r, :].astype(F32)
        sq[r, :] = lane_fold(x * x)
        xl[r, :] = (x * eg_ref[:, mine_f]).astype(BF16)
        return c

    for i in range(parts):
        copy_tok[i].wait()
        lax.fori_loop(i * prow // blk, (i + 1) * prow // blk, scale_local, 0)

    pl.semaphore_wait(barrier, npsg - 1 + npb - 1 + 1)

    def to_other(src, dst, i):
        return pltpu.make_async_remote_copy(
            src_ref=src, dst_ref=dst, send_sem=tsend.at[i], recv_sem=trecv.at[i],
            device_id={"tp": other}, device_id_type=MESH,
        )

    send_sq = to_other(sq, sqp, 0)
    send_tok = to_other(xl, xr, 1)
    send_wo = to_other(wo_hbm.at[:, peer_f], wo.at[1], 2)
    send_tok.start()
    send_sq.start()

    def to_pb(k, src, dst, base):
        to = lax.rem(pb + k, npb)
        return pltpu.make_async_remote_copy(
            src_ref=src.at[to], dst_ref=dst.at[pb], send_sem=psend.at[base + k - 1], recv_sem=precv.at[base + k - 1],
            device_id={"pb": to}, device_id_type=MESH,
        )

    def to_psg(k, src, dst, ss, rs):
        return pltpu.make_async_remote_copy(
            src_ref=src, dst_ref=dst, send_sem=ss.at[k - 1], recv_sem=rs.at[k - 1],
            device_id={"psg": lax.rem(psg + k, npsg)}, device_id_type=MESH,
        )

    send_dn = [to_pb(k, dn, dnr, 0) for k in range(1, npb)]
    for s in send_dn:
        s.start()
    dnr[pb] = dn[pb]

    nt = min(512, cols)
    for w in range(3):
        copy_w[w][0].wait()

        def first_half(j, c):
            t = pl.ds(pl.multiple_of(j * nt, nt), nt)
            acc[w, :, t] = nn_dot(xl[...], wbuf[w, 0, :, t])
            return c

        lax.fori_loop(0, cols // nt, first_half, 0)
        if w == 1:
            for s in send_dn:
                s.wait()
            copy_dec.wait()
            dqp[...] = nn_dot(dnr[...].reshape(npb * 8, depth).astype(BF16), decw[...]).reshape(npb, 8, cols)
            send_dq = [to_pb(k, dqp, dqr, npb - 1) for k in range(1, npb)]
            for s in send_dq:
                s.start()
            dqr[pb] = dqp[pb]

    copy_cv = [
        pltpu.make_async_copy(cv_hbm.at[mine_f, :], wbuf.at[0, 0], lsem.at[0]),
        pltpu.make_async_copy(cv_hbm.at[peer_f, :], wbuf.at[1, 0], lsem.at[9]),
    ]
    send_tok.wait()
    send_wo.start()
    send_sq.wait()

    def inverse(i, c):
        r = pl.ds(pl.multiple_of(i * blk, blk), blk)
        ms = jnp.sum(sq[r, :] + sqp[r, :], axis=-1, keepdims=True) * (1.0 / width) + EPS
        inv[r, :] = jnp.broadcast_to(lax.rsqrt(ms), (blk, 128))
        return c

    lax.fori_loop(0, rows // blk, inverse, 0)

    for w in range(3):
        copy_w[w][1].wait()

        def second_half(j, c):
            t = pl.ds(pl.multiple_of(j * nt, nt), nt)
            scale = jnp.concatenate([inv[...]] * (nt // 128), axis=1)
            qkv[w, :, t] = ((acc[w, :, t] + nn_dot(xr[...], wbuf[w, 1, :, t])) * scale).astype(BF16)
            return c

        lax.fori_loop(0, cols // nt, second_half, 0)
        if w == 0:
            copy_cv[0].start()
            copy_cv[1].start()
            for s in send_dq:
                s.wait()
            dq = dqr[0]
            for j in range(1, npb):
                dq = dq + dqr[j]
            dq = dq.astype(BF16).astype(F32)
            head_of = lax.broadcasted_iota(jnp.int32, (heads, cols), 1) // DH
            head_row = lax.broadcasted_iota(jnp.int32, (heads, cols), 0)
            for b in range(beams):
                bd[b * heads : (b + 1) * heads, :] = jnp.where(head_of == head_row, dq[b : b + 1, :], 0.0).astype(BF16)
            for f, c in enumerate((tp, other)):
                copy_ck[f].wait()
                gain = fg_ref[:, pl.ds(pl.multiple_of(c * half + psg * fc, fc), fc)]
                gpart[f] = (nt_dot(bd[...], ckb[f]) * gain).astype(BF16)

            def start_gq(k, c):
                to_psg(k, gpart, gqa.at[:, psg], gsend, grecv).start()
                return c

            lax.fori_loop(1, npsg, start_gq, 0)
            gqa[:, psg] = gpart[...]

    lane = lax.broadcasted_iota(jnp.int32, (plen, 128), 1)
    low = lane < DH
    slot = lax.broadcasted_iota(jnp.int32, (1, plen), 1)
    groups = cols // 256
    send_att = []
    for g in range(groups):
        for p in range(passages):
            key_live = slot < len_ref[0, psg * passages + p]
            r = slice(p * plen, (p + 1) * plen)
            for pair in range(2):
                t = slice(g * 256 + pair * 128, g * 256 + pair * 128 + 128)
                q = qkv[0, r, t]
                zero = jnp.zeros_like(q)
                q2 = jnp.concatenate([jnp.where(low, q, zero), jnp.where(low, zero, q)], axis=0)
                s = jnp.where(key_live, nt_dot(q2, qkv[1, r, t]), NEGATIVE)
                e = jnp.exp2((s - jnp.max(s, axis=-1, keepdims=True)) * (SCALE * LOG2E))
                den = jnp.sum(e, axis=-1, keepdims=True)
                o = nn_dot(e.astype(BF16), qkv[2, r, t]) / den
                att[r, t] = jnp.where(low, o[:plen], o[plen:]).astype(BF16)
        t = slice(g * 256, g * 256 + 256)
        s = to_other(att.at[:, t], attp.at[:, t], 3 + g)
        s.start()
        send_att.append(s)

    mine_h = pl.ds(pl.multiple_of(tp * hb, hb), hb)
    peer_h = pl.ds(pl.multiple_of(other * hb, hb), hb)

    def wait_gq(k, c):
        to_psg(k, gpart, gqa.at[:, psg], gsend, grecv).wait()
        return c

    lax.fori_loop(1, npsg, wait_gq, 0)
    send_gq = to_other(gqa.at[1], gqp, 3 + groups)
    send_gq.start()
    for i in range(npsg):
        gq[mine_h, i * fc : (i + 1) * fc] = gqa[0, i]

    copy_wo.wait()

    def out_own(j, c):
        t = pl.ds(pl.multiple_of(j * nt, nt), nt)
        per = cols // nt
        acc[j // per, :, pl.ds(pl.multiple_of((j % per) * nt, nt), nt)] = nn_dot(att[...], wo[0, :, t])
        return c

    lax.fori_loop(0, half // nt, out_own, 0)
    for s in send_att:
        s.wait()
    send_gq.wait()
    for i in range(npsg):
        gq[peer_h, i * fc : (i + 1) * fc] = gqp[i]
    send_wo.wait()
    sq[...] = jnp.zeros_like(sq)
    sc[0 : 2 * hb, :] = jnp.zeros((2 * hb, rows), F32)

    def out_peer(j, c):
        t = pl.ds(pl.multiple_of(j * nt, nt), nt)
        per = cols // nt
        a = acc[j // per, :, pl.ds(pl.multiple_of((j % per) * nt, nt), nt)]
        e = (tok[:, t].astype(F32) + (a + nn_dot(attp[...], wo[1, :, t]))).astype(BF16)
        enc[:, t] = e
        wide = e.astype(F32)
        sq[...] += lane_fold(wide * wide)
        sc[0 : 2 * hb, :] += nt_dot(gq[:, t], e)
        return c

    lax.fori_loop(0, half // nt, out_peer, 0)
    copy_enc = pltpu.make_async_copy(enc, enc_hbm, lsem.at[13])
    sc[2 * hb : 2 * hb + 8, :] = jnp.broadcast_to(jnp.sum(jnp.transpose(sq[...]), axis=0, keepdims=True), (8, rows))
    send_sc = to_other(sc, scp, 4 + groups)
    send_sc.start()
    copy_enc.start()
    send_sc.wait()

    both = sc[...] + scp[...]
    x = both[2 * hb : 2 * hb + 1, :] * (1.0 / width) + EPS
    iv = lax.rsqrt(x)
    at = lax.broadcasted_iota(jnp.int32, (1, rows), 1)
    limit = jnp.zeros((1, rows), jnp.int32) + len_ref[0, psg * passages]
    for p in range(1, passages):
        limit = jnp.where(at >= p * plen, p * plen + len_ref[0, psg * passages + p], limit)
    live = at < limit
    s = jnp.where(live, both[0 : 2 * hb, :] * (iv * SCALE), NEGATIVE)
    peak = jnp.max(s, axis=1, keepdims=True)
    e = jnp.where(live, jnp.exp2((s - peak) * LOG2E), 0.0)
    wt = (e * iv).astype(BF16)
    total = jnp.sum(wt.astype(F32) * (x * iv), axis=1, keepdims=True)

    def mixed(j, c):
        t = pl.ds(pl.multiple_of(j * nt, nt), nt)
        gain = fg_ref[:, pl.ds(pl.multiple_of(tp * half + j * nt, nt), nt)]
        mix[:, t] = (nn_dot(wt, enc[:, t]) * gain).astype(BF16)
        return c

    lax.fori_loop(0, half // nt, mixed, 0)
    send_mix = to_other(mix.at[peer_h, :], mixp, 5 + groups)
    send_mix.start()
    first = lax.broadcasted_iota(jnp.int32, (2 * hb, 128), 1) == 0
    stat[...] = jnp.transpose(jnp.where(first, peak, total))[0:8, :]

    def start_stat(k, c):
        to_psg(k, stat, stats.at[psg], ssend, srecv).start()
        return c

    lax.fori_loop(1, npsg, start_stat, 0)
    stats[psg] = stat[...]


    ct = 256
    r_head = lax.rem(lax.broadcasted_iota(jnp.int32, (hb, ct), 0), heads)
    c_head = lax.broadcasted_iota(jnp.int32, (hb, ct), 1) // DH

    copy_cv[0].wait()
    for g in range(cols // ct):
        t = slice(g * ct, (g + 1) * ct)
        acc[0, 0:hb, t] = nn_dot(mix[mine_h, :], wbuf[0, 0, :, t])
    copy_cv[1].wait()
    send_mix.wait()
    for g in range(cols // ct):
        t = slice(g * ct, (g + 1) * ct)
        m = acc[0, 0:hb, t] + nn_dot(mixp[...], wbuf[1, 0, :, t])
        m = jnp.where(r_head == c_head + g * (ct // DH), m, 0.0)
        for b in range(beams):
            r = g * beams + b
            ctf[r : r + 1, :] = jnp.sum(m[b * heads : (b + 1) * heads], axis=0, keepdims=True)
    ctp[...] = ctf[...].astype(BF16)

    def start_ctx(k, c):
        to_psg(k, ctp, cts.at[psg], csend, crecv).start()
        return c

    lax.fori_loop(1, npsg, start_ctx, 0)
    cts[psg] = ctp[...]

    def wait_stat(k, c):
        to_psg(k, stat, stats.at[psg], ssend, srecv).wait()
        return c

    lax.fori_loop(1, npsg, wait_stat, 0)
    peaks = stats[:, 0:1, :]
    factor = jnp.exp2((peaks - jnp.max(peaks, axis=0, keepdims=True)) * LOG2E)
    factor = factor / jnp.sum(stats[:, 1:2, :] * factor, axis=0, keepdims=True)
    nr = beams * cols // ct
    per = ct // DH
    c_of = lax.broadcasted_iota(jnp.int32, (nr, 2 * hb), 1) - tp * hb
    r_of = lax.broadcasted_iota(jnp.int32, (nr, 2 * hb), 0)
    own = (c_of >= 0) & (c_of < hb) & (lax.div(c_of, heads) == lax.rem(r_of, beams))
    own = own & (lax.div(lax.rem(c_of, heads), per) == lax.div(r_of, beams))
    own = jnp.where(own, 1.0, 0.0)
    spread = (factor * own[None]).reshape(npsg * nr, 2 * hb)
    coarse = spread.astype(BF16)
    fine = (spread - coarse.astype(F32)).astype(BF16)
    one = lax.rem(lax.broadcasted_iota(jnp.int32, (2 * hb, ct), 0), per) == lax.broadcasted_iota(jnp.int32, (2 * hb, ct), 1) // DH
    one = jnp.where(one, 1.0, 0.0).astype(BF16)
    xs[...] = (nn_dot(coarse, one) + nn_dot(fine, one)).reshape(npsg, nr, ct)

    def wait_ctx(k, c):
        to_psg(k, ctp, cts.at[psg], csend, crecv).wait()
        return c

    lax.fori_loop(1, npsg, wait_ctx, 0)
    whole = jnp.sum(cts[...].astype(F32) * xs[...], axis=0)
    for g in range(cols // ct):
        ctx_ref[:, g * ct : (g + 1) * ct] = whole[g * beams : (g + 1) * beams, :]
    copy_enc.wait()


def writer(enc_hbm, ctx_in, enc_out, ctx_out, held, sem_in, sem_out):
    n = sem_in.shape[0]
    rows = enc_hbm.shape[0] // n
    part = [pl.ds(i * rows, rows) for i in range(n)]
    ins = [pltpu.make_async_copy(enc_hbm.at[p, :], held.at[p, :], sem_in.at[i]) for i, p in enumerate(part)]
    outs = [pltpu.make_async_copy(held.at[p, :], enc_out.at[p, :], sem_out.at[i]) for i, p in enumerate(part)]
    for c in ins:
        c.start()
    ctx_out[...] = ctx_in[...]
    for i in range(n):
        ins[i].wait()
        outs[i].start()
    for c in outs:
        c.wait()


def per_device(
    tokens, lengths, enc_gain, w_query, w_key, w_value, w_out, final_gain, cross_key, cross_value,
    beam_states, parents, dec_gain, dec_query,
):
    questions, passages, plen, half = tokens.shape
    rows = questions * passages * plen
    cols = w_query.shape[1]
    heads = cols // DH
    beams = beam_states.shape[1]
    hb = heads * beams
    width = 2 * half
    npsg, npb = lax.axis_size("psg"), lax.axis_size("pb")
    groups = cols // 256
    vmem = pl.BlockSpec(memory_space=pltpu.VMEM)
    smem = pl.BlockSpec(memory_space=pltpu.SMEM)
    hbm = pl.BlockSpec(memory_space=pl.ANY)
    V, D = pltpu.VMEM, pltpu.SemaphoreType.DMA
    encoded, context = pl.pallas_call(
        functools.partial(body, (npsg, npb)),
        out_shape=(
            jax.ShapeDtypeStruct((rows, half), BF16),
            jax.ShapeDtypeStruct((beams, cols), F32),
        ),
        in_specs=[hbm, smem, vmem, hbm, hbm, hbm, hbm, vmem, hbm, hbm, vmem, smem, vmem, hbm],
        out_specs=(hbm, vmem),
        scratch_shapes=[
            V((rows, half), BF16),
            V((rows, half), BF16),
            V((rows, half), BF16),
            V((3, 2, half, cols), BF16),
            V((2, cols, half), BF16),
            V((3, rows, cols), F32),
            V((3, rows, cols), BF16),
            V((rows, cols), BF16),
            V((rows, cols), BF16),
            V((rows, half), BF16),
            V((width // npb, cols), BF16),
            V((rows, 128), F32),
            V((rows, 128), F32),
            V((rows, 128), F32),
            V((2 * hb, half), BF16),
            V((2 * hb + 8, rows), F32),
            V((2 * hb + 8, rows), F32),
            V((2 * hb, half), BF16),
            V((hb, half), BF16),
            V((hb, cols), BF16),
            V((npb, 8, width // npb), F32),
            V((npb, 8, width // npb), F32),
            V((npb, 8, cols), F32),
            V((npb, 8, cols), F32),
            V((8, 2 * hb), F32),
            V((npsg, 8, 2 * hb), F32),
            V((beams * cols // 256, 256), F32),
            V((beams * cols // 256, 256), BF16),
            V((npsg, beams * cols // 256, 256), BF16),
            V((npsg, beams * cols // 256, 256), F32),
            V((2, half // npsg, cols), BF16),
            V((2, hb, half // npsg), BF16),
            V((2, npsg, hb, half // npsg), BF16),
            V((npsg, hb, half // npsg), BF16),
            D((16,)),
            D((6 + groups,)),
            D((6 + groups,)),
            D((2 * (npb - 1),)),
            D((2 * (npb - 1),)),
            D((npsg - 1,)),
            D((npsg - 1,)),
            D((npsg - 1,)),
            D((npsg - 1,)),
            D((npsg - 1,)),
            D((npsg - 1,)),
        ],
        compiler_params=pltpu.CompilerParams(
            collective_id=0, has_side_effects=True, vmem_limit_bytes=60 * 2**20
        ),
    )(
        tokens.reshape(rows, half), lengths, enc_gain.reshape(1, width), w_query, w_key, w_value, w_out,
        final_gain.reshape(1, width), cross_key, cross_value, beam_states.reshape(beams, width), parents,
        dec_gain.reshape(1, width), dec_query,
    )
    encoded, context = pl.pallas_call(
        writer,
        out_shape=(
            jax.ShapeDtypeStruct((rows, half), BF16),
            jax.ShapeDtypeStruct((beams, cols), F32),
        ),
        in_specs=[hbm, vmem],
        out_specs=(hbm, vmem),
        scratch_shapes=[V((rows, half), BF16), D((8,)), D((8,))],
    )(encoded, context)
    return (
        encoded.reshape(questions, passages, plen, half),
        context.reshape(questions, beams, cols),
    )


def solution(mesh):
    in_specs = (
        P("pb", "psg", None, "tp"),
        P("pb", None),
        P(),
        P(None, "tp"),
        P(None, "tp"),
        P(None, "tp"),
        P("tp", None),
        P(),
        P(None, "tp"),
        P(None, "tp"),
        P("pb", None, None),
        P("pb", None),
        P(),
        P("pb", "tp"),
    )
    out_specs = (P("pb", "psg", None, "tp"), P("pb", None, "tp"))
    return jax.shard_map(
        per_device, mesh=mesh, in_specs=in_specs, out_specs=out_specs, check_vma=False
    )
```

```python
import functools

import jax
import jax.numpy as jnp
from jax import lax
from jax.experimental import pallas as pl
from jax.experimental.pallas import tpu as pltpu
from jax.sharding import PartitionSpec as P

DH = 64
EPS = 1e-06
SCALE = 0.125
LOG2E = 1.4426950408889634
NEGATIVE = -1e30
MESH = pl.DeviceIdType.MESH
F32 = jnp.float32
BF16 = jnp.bfloat16


def nt_dot(a, b):
    return lax.dot_general(a, b, (((1,), (1,)), ((), ())), preferred_element_type=F32)


def nn_dot(a, b):
    return jnp.dot(a, b, preferred_element_type=F32)


def lane_fold(x):
    total = x[:, :128]
    for i in range(1, x.shape[1] // 128):
        total = total + x[:, i * 128 : (i + 1) * 128]
    return total


def body(
    sizes,
    tok_hbm, len_ref, eg_ref, wq_hbm, wk_hbm, wv_hbm, wo_hbm, fg_ref, ck_hbm, cv_hbm, beam_ref, par_ref, dg_ref, dec_hbm,
    enc_hbm, ctx_ref,
    tok, xl, xr, wbuf, wo, acc, qkv, att, attp, decw,
    sq, sqp, inv, gq, sc, scp, mix, mixp, bd, dn, dnr, dqp, dqr, stat, stats, ctf, ctp, cts, xs, ckb, gpart, gqa, gqp,
    lsem, tsend, trecv, psend, precv, ssend, srecv, csend, crecv, gsend, grecv,
):
    npsg, npb = sizes
    enc = xl
    rows, half = tok.shape
    width = 2 * half
    cols = qkv.shape[2]
    heads = cols // DH
    beams = beam_ref.shape[0]
    hb = heads * beams
    plen = 256
    passages = rows // plen
    tp = lax.axis_index("tp")
    psg = lax.axis_index("psg")
    pb = lax.axis_index("pb")
    other = 1 - tp
    mine_f = pl.ds(pl.multiple_of(tp * half, half), half)
    peer_f = pl.ds(pl.multiple_of(other * half, half), half)

    barrier = pltpu.get_barrier_semaphore()
    pl.semaphore_signal(barrier, inc=1, device_id={"tp": other}, device_id_type=MESH)

    def hello_psg(k, c):
        pl.semaphore_signal(barrier, inc=1, device_id={"psg": lax.rem(psg + k, npsg)}, device_id_type=MESH)
        return c

    lax.fori_loop(1, npsg, hello_psg, 0)
    for k in range(1, npb):
        pl.semaphore_signal(barrier, inc=1, device_id={"pb": lax.rem(pb + k, npb)}, device_id_type=MESH)

    parts = 4
    prow = rows // parts
    copy_tok = [
        pltpu.make_async_copy(tok_hbm.at[pl.ds(i * prow, prow), :], tok.at[pl.ds(i * prow, prow), :], lsem.at[10 + i])
        for i in range(parts)
    ]
    for c in copy_tok:
        c.start()
    w_hbm = (wq_hbm, wk_hbm, wv_hbm)
    copy_w = [[None, None] for _ in range(3)]
    for h, part in enumerate((mine_f, peer_f)):
        for w in range(3):
            copy_w[w][h] = pltpu.make_async_copy(w_hbm[w].at[part, :], wbuf.at[w, h], lsem.at[1 + 2 * w + h])
    copy_dec = pltpu.make_async_copy(dec_hbm, decw, lsem.at[7])
    copy_wo = pltpu.make_async_copy(wo_hbm.at[:, mine_f], wo.at[0], lsem.at[8])
    for w in range(3):
        copy_w[w][0].start()
    copy_dec.start()
    fc = half // npsg
    copy_ck = [
        pltpu.make_async_copy(ck_hbm.at[pl.ds(pl.multiple_of(c * half + psg * fc, fc), fc), :], ckb.at[f], lsem.at[14 + f])
        for f, c in enumerate((tp, other))
    ]
    for c in copy_ck:
        c.start()
    for w in range(3):
        copy_w[w][1].start()
    copy_wo.start()

    chosen = []
    for b in range(beams):
        row = jnp.zeros((1, width), F32)
        for c in range(beams):
            row = row + (par_ref[0, b] == c).astype(F32) * beam_ref[c : c + 1, :].astype(F32)
        chosen.append(row)
    depth = width // npb
    for b in range(beams):
        row = chosen[b]
        ms = jnp.sum(row * row, axis=-1, keepdims=True) * (1.0 / width) + EPS
        row = (row * lax.rsqrt(ms) * dg_ref[...]).astype(BF16).astype(F32)
        for j in range(npb):
            dn[j, b : b + 1, :] = row[:, j * depth : (j + 1) * depth]
    for j in range(npb):
        dn[j, beams:8, :] = jnp.zeros((8 - beams, depth), F32)

    blk = 32

    def scale_local(i, c):
        r = pl.ds(pl.multiple_of(i * blk, blk), blk)
        x = tok[r, :].astype(F32)
        sq[r, :] = lane_fold(x * x)
        xl[r, :] = (x * eg_ref[:, mine_f]).astype(BF16)
        return c

    for i in range(parts):
        copy_tok[i].wait()
        lax.fori_loop(i * prow // blk, (i + 1) * prow // blk, scale_local, 0)

    pl.semaphore_wait(barrier, npsg - 1 + npb - 1 + 1)

    def to_other(src, dst, i):
        return pltpu.make_async_remote_copy(
            src_ref=src, dst_ref=dst, send_sem=tsend.at[i], recv_sem=trecv.at[i],
            device_id={"tp": other}, device_id_type=MESH,
        )

    send_sq = to_other(sq, sqp, 0)
    send_tok = to_other(xl, xr, 1)
    send_wo = to_other(wo_hbm.at[:, peer_f], wo.at[1], 2)
    send_tok.start()
    send_sq.start()

    def to_pb(k, src, dst, base):
        to = lax.rem(pb + k, npb)
        return pltpu.make_async_remote_copy(
            src_ref=src.at[to], dst_ref=dst.at[pb], send_sem=psend.at[base + k - 1], recv_sem=precv.at[base + k - 1],
            device_id={"pb": to}, device_id_type=MESH,
        )

    def to_psg(k, src, dst, ss, rs):
        return pltpu.make_async_remote_copy(
            src_ref=src, dst_ref=dst, send_sem=ss.at[k - 1], recv_sem=rs.at[k - 1],
            device_id={"psg": lax.rem(psg + k, npsg)}, device_id_type=MESH,
        )

    send_dn = [to_pb(k, dn, dnr, 0) for k in range(1, npb)]
    for s in send_dn:
        s.start()
    dnr[pb] = dn[pb]

    nt = min(512, cols)
    for w in range(3):
        copy_w[w][0].wait()

        def first_half(j, c):
            t = slice(j * nt, j * nt + nt)
            acc[w, :, t] = nn_dot(xl[...], wbuf[w, 0, :, t])
            return c

        for j in range(cols // nt):
            first_half(j, 0)
        if w == 1:
            for s in send_dn:
                s.wait()
            copy_dec.wait()
            dqp[...] = nn_dot(dnr[...].reshape(npb * 8, depth).astype(BF16), decw[...]).reshape(npb, 8, cols)
            send_dq = [to_pb(k, dqp, dqr, npb - 1) for k in range(1, npb)]
            for s in send_dq:
                s.start()
            dqr[pb] = dqp[pb]

    copy_cv = [
        pltpu.make_async_copy(cv_hbm.at[mine_f, :], wbuf.at[0, 0], lsem.at[0]),
        pltpu.make_async_copy(cv_hbm.at[peer_f, :], wbuf.at[1, 0], lsem.at[9]),
    ]
    send_tok.wait()
    send_wo.start()
    send_sq.wait()

    def inverse(i, c):
        r = pl.ds(pl.multiple_of(i * blk, blk), blk)
        ms = jnp.sum(sq[r, :] + sqp[r, :], axis=-1, keepdims=True) * (1.0 / width) + EPS
        inv[r, :] = jnp.broadcast_to(lax.rsqrt(ms), (blk, 128))
        return c

    lax.fori_loop(0, rows // blk, inverse, 0)

    for w in range(3):
        copy_w[w][1].wait()

        def second_half(j, c):
            t = slice(j * nt, j * nt + nt)
            scale = jnp.concatenate([inv[...]] * (nt // 128), axis=1)
            qkv[w, :, t] = ((acc[w, :, t] + nn_dot(xr[...], wbuf[w, 1, :, t])) * scale).astype(BF16)
            return c

        for j in range(cols // nt):
            second_half(j, 0)
        if w == 0:
            copy_cv[0].start()
            copy_cv[1].start()
            for s in send_dq:
                s.wait()
            dq = dqr[0]
            for j in range(1, npb):
                dq = dq + dqr[j]
            dq = dq.astype(BF16).astype(F32)
            head_of = lax.broadcasted_iota(jnp.int32, (heads, cols), 1) // DH
            head_row = lax.broadcasted_iota(jnp.int32, (heads, cols), 0)
            for b in range(beams):
                bd[b * heads : (b + 1) * heads, :] = jnp.where(head_of == head_row, dq[b : b + 1, :], 0.0).astype(BF16)
            for f, c in enumerate((tp, other)):
                copy_ck[f].wait()
                gain = fg_ref[:, pl.ds(pl.multiple_of(c * half + psg * fc, fc), fc)]
                gpart[f] = (nt_dot(bd[...], ckb[f]) * gain).astype(BF16)

            def start_gq(k, c):
                to_psg(k, gpart, gqa.at[:, psg], gsend, grecv).start()
                return c

            lax.fori_loop(1, npsg, start_gq, 0)
            gqa[:, psg] = gpart[...]

    lane = lax.broadcasted_iota(jnp.int32, (plen, 128), 1)
    low = lane < DH
    slot = lax.broadcasted_iota(jnp.int32, (1, plen), 1)
    groups = cols // 256
    send_att = []
    for g in range(groups):
        for p in range(passages):
            key_live = slot < len_ref[0, psg * passages + p]
            r = slice(p * plen, (p + 1) * plen)
            for pair in range(2):
                t = slice(g * 256 + pair * 128, g * 256 + pair * 128 + 128)
                q = qkv[0, r, t]
                zero = jnp.zeros_like(q)
                q2 = jnp.concatenate([jnp.where(low, q, zero), jnp.where(low, zero, q)], axis=0)
                s = jnp.where(key_live, nt_dot(q2, qkv[1, r, t]), NEGATIVE)
                e = jnp.exp2((s - jnp.max(s, axis=-1, keepdims=True)) * (SCALE * LOG2E))
                den = jnp.sum(e, axis=-1, keepdims=True)
                o = nn_dot(e.astype(BF16), qkv[2, r, t]) / den
                att[r, t] = jnp.where(low, o[:plen], o[plen:]).astype(BF16)
        t = slice(g * 256, g * 256 + 256)
        s = to_other(att.at[:, t], attp.at[:, t], 3 + g)
        s.start()
        send_att.append(s)

    mine_h = pl.ds(pl.multiple_of(tp * hb, hb), hb)
    peer_h = pl.ds(pl.multiple_of(other * hb, hb), hb)

    def wait_gq(k, c):
        to_psg(k, gpart, gqa.at[:, psg], gsend, grecv).wait()
        return c

    lax.fori_loop(1, npsg, wait_gq, 0)
    send_gq = to_other(gqa.at[1], gqp, 3 + groups)
    send_gq.start()
    for i in range(npsg):
        gq[mine_h, i * fc : (i + 1) * fc] = gqa[0, i]

    copy_wo.wait()

    def out_own(j, c):
        t = slice(j * nt, j * nt + nt)
        per = cols // nt
        acc[j // per, :, slice((j % per) * nt, (j % per) * nt + nt)] = nn_dot(att[...], wo[0, :, t])
        return c

    for j in range(half // nt):
        out_own(j, 0)
    for s in send_att:
        s.wait()
    send_gq.wait()
    for i in range(npsg):
        gq[peer_h, i * fc : (i + 1) * fc] = gqp[i]
    send_wo.wait()
    sq[...] = jnp.zeros_like(sq)
    sc[0 : 2 * hb, :] = jnp.zeros((2 * hb, rows), F32)

    def out_peer(j, c):
        t = slice(j * nt, j * nt + nt)
        per = cols // nt
        a = acc[j // per, :, slice((j % per) * nt, (j % per) * nt + nt)]
        e = (tok[:, t].astype(F32) + (a + nn_dot(attp[...], wo[1, :, t]))).astype(BF16)
        enc[:, t] = e
        wide = e.astype(F32)
        sq[...] += lane_fold(wide * wide)
        sc[0 : 2 * hb, :] += nt_dot(gq[:, t], e)
        return c

    for j in range(half // nt):
        out_peer(j, 0)
    copy_enc = pltpu.make_async_copy(enc, enc_hbm, lsem.at[13])
    sc[2 * hb : 2 * hb + 8, :] = jnp.broadcast_to(jnp.sum(jnp.transpose(sq[...]), axis=0, keepdims=True), (8, rows))
    send_sc = to_other(sc, scp, 4 + groups)
    send_sc.start()
    copy_enc.start()
    send_sc.wait()

    both = sc[...] + scp[...]
    x = both[2 * hb : 2 * hb + 1, :] * (1.0 / width) + EPS
    iv = lax.rsqrt(x)
    at = lax.broadcasted_iota(jnp.int32, (1, rows), 1)
    limit = jnp.zeros((1, rows), jnp.int32) + len_ref[0, psg * passages]
    for p in range(1, passages):
        limit = jnp.where(at >= p * plen, p * plen + len_ref[0, psg * passages + p], limit)
    live = at < limit
    s = jnp.where(live, both[0 : 2 * hb, :] * (iv * SCALE), NEGATIVE)
    peak = jnp.max(s, axis=1, keepdims=True)
    e = jnp.where(live, jnp.exp2((s - peak) * LOG2E), 0.0)
    wt = (e * iv).astype(BF16)
    total = jnp.sum(wt.astype(F32) * (x * iv), axis=1, keepdims=True)

    def mixed(j, c):
        t = pl.ds(pl.multiple_of(j * nt, nt), nt)
        gain = fg_ref[:, pl.ds(pl.multiple_of(tp * half + j * nt, nt), nt)]
        mix[:, t] = (nn_dot(wt, enc[:, t]) * gain).astype(BF16)
        return c

    lax.fori_loop(0, half // nt, mixed, 0)
    send_mix = to_other(mix.at[peer_h, :], mixp, 5 + groups)
    send_mix.start()
    first = lax.broadcasted_iota(jnp.int32, (2 * hb, 128), 1) == 0
    stat[...] = jnp.transpose(jnp.where(first, peak, total))[0:8, :]

    def start_stat(k, c):
        to_psg(k, stat, stats.at[psg], ssend, srecv).start()
        return c

    lax.fori_loop(1, npsg, start_stat, 0)
    stats[psg] = stat[...]


    ct = 256
    r_head = lax.rem(lax.broadcasted_iota(jnp.int32, (hb, ct), 0), heads)
    c_head = lax.broadcasted_iota(jnp.int32, (hb, ct), 1) // DH

    copy_cv[0].wait()
    for g in range(cols // ct):
        t = slice(g * ct, (g + 1) * ct)
        acc[0, 0:hb, t] = nn_dot(mix[mine_h, :], wbuf[0, 0, :, t])
    copy_cv[1].wait()
    send_mix.wait()
    for g in range(cols // ct):
        t = slice(g * ct, (g + 1) * ct)
        m = acc[0, 0:hb, t] + nn_dot(mixp[...], wbuf[1, 0, :, t])
        m = jnp.where(r_head == c_head + g * (ct // DH), m, 0.0)
        for b in range(beams):
            r = g * beams + b
            ctf[r : r + 1, :] = jnp.sum(m[b * heads : (b + 1) * heads], axis=0, keepdims=True)
    ctp[...] = ctf[...].astype(BF16)

    def start_ctx(k, c):
        to_psg(k, ctp, cts.at[psg], csend, crecv).start()
        return c

    lax.fori_loop(1, npsg, start_ctx, 0)
    cts[psg] = ctp[...]

    def wait_stat(k, c):
        to_psg(k, stat, stats.at[psg], ssend, srecv).wait()
        return c

    lax.fori_loop(1, npsg, wait_stat, 0)
    peaks = stats[:, 0:1, :]
    factor = jnp.exp2((peaks - jnp.max(peaks, axis=0, keepdims=True)) * LOG2E)
    factor = factor / jnp.sum(stats[:, 1:2, :] * factor, axis=0, keepdims=True)
    nr = beams * cols // ct
    per = ct // DH
    c_of = lax.broadcasted_iota(jnp.int32, (nr, 2 * hb), 1) - tp * hb
    r_of = lax.broadcasted_iota(jnp.int32, (nr, 2 * hb), 0)
    own = (c_of >= 0) & (c_of < hb) & (lax.div(c_of, heads) == lax.rem(r_of, beams))
    own = own & (lax.div(lax.rem(c_of, heads), per) == lax.div(r_of, beams))
    own = jnp.where(own, 1.0, 0.0)
    spread = (factor * own[None]).reshape(npsg * nr, 2 * hb)
    coarse = spread.astype(BF16)
    fine = (spread - coarse.astype(F32)).astype(BF16)
    one = lax.rem(lax.broadcasted_iota(jnp.int32, (2 * hb, ct), 0), per) == lax.broadcasted_iota(jnp.int32, (2 * hb, ct), 1) // DH
    one = jnp.where(one, 1.0, 0.0).astype(BF16)
    xs[...] = (nn_dot(coarse, one) + nn_dot(fine, one)).reshape(npsg, nr, ct)

    def wait_ctx(k, c):
        to_psg(k, ctp, cts.at[psg], csend, crecv).wait()
        return c

    lax.fori_loop(1, npsg, wait_ctx, 0)
    whole = jnp.sum(cts[...].astype(F32) * xs[...], axis=0)
    for g in range(cols // ct):
        ctx_ref[:, g * ct : (g + 1) * ct] = whole[g * beams : (g + 1) * beams, :]
    copy_enc.wait()


def writer(enc_hbm, ctx_hbm, enc_out, ctx_out, held, ctx, sem_in, sem_out):
    n = sem_in.shape[0] - 1
    rows = enc_hbm.shape[0] // n
    part = [pl.ds(i * rows, rows) for i in range(n)]
    ins = [pltpu.make_async_copy(enc_hbm.at[p, :], held.at[p, :], sem_in.at[i]) for i, p in enumerate(part)]
    ins.append(pltpu.make_async_copy(ctx_hbm, ctx, sem_in.at[n]))
    outs = [pltpu.make_async_copy(held.at[p, :], enc_out.at[p, :], sem_out.at[i]) for i, p in enumerate(part)]
    outs.append(pltpu.make_async_copy(ctx, ctx_out, sem_out.at[n]))
    for c in ins:
        c.start()
    for i in range(n + 1):
        ins[i].wait()
        outs[i].start()
    for c in outs:
        c.wait()


def per_device(
    tokens, lengths, enc_gain, w_query, w_key, w_value, w_out, final_gain, cross_key, cross_value,
    beam_states, parents, dec_gain, dec_query,
):
    questions, passages, plen, half = tokens.shape
    rows = questions * passages * plen
    cols = w_query.shape[1]
    heads = cols // DH
    beams = beam_states.shape[1]
    hb = heads * beams
    width = 2 * half
    npsg, npb = lax.axis_size("psg"), lax.axis_size("pb")
    groups = cols // 256
    vmem = pl.BlockSpec(memory_space=pltpu.VMEM)
    smem = pl.BlockSpec(memory_space=pltpu.SMEM)
    hbm = pl.BlockSpec(memory_space=pl.ANY)
    V, D = pltpu.VMEM, pltpu.SemaphoreType.DMA
    encoded, context = pl.pallas_call(
        functools.partial(body, (npsg, npb)),
        out_shape=(
            jax.ShapeDtypeStruct((rows, half), BF16),
            jax.ShapeDtypeStruct((beams, cols), F32),
        ),
        in_specs=[hbm, smem, vmem, hbm, hbm, hbm, hbm, vmem, hbm, hbm, vmem, smem, vmem, hbm],
        out_specs=(hbm, vmem),
        scratch_shapes=[
            V((rows, half), BF16),
            V((rows, half), BF16),
            V((rows, half), BF16),
            V((3, 2, half, cols), BF16),
            V((2, cols, half), BF16),
            V((3, rows, cols), F32),
            V((3, rows, cols), BF16),
            V((rows, cols), BF16),
            V((rows, cols), BF16),
            V((width // npb, cols), BF16),
            V((rows, 128), F32),
            V((rows, 128), F32),
            V((rows, 128), F32),
            V((2 * hb, half), BF16),
            V((2 * hb + 8, rows), F32),
            V((2 * hb + 8, rows), F32),
            V((2 * hb, half), BF16),
            V((hb, half), BF16),
            V((hb, cols), BF16),
            V((npb, 8, width // npb), F32),
            V((npb, 8, width // npb), F32),
            V((npb, 8, cols), F32),
            V((npb, 8, cols), F32),
            V((8, 2 * hb), F32),
            V((npsg, 8, 2 * hb), F32),
            V((beams * cols // 256, 256), F32),
            V((beams * cols // 256, 256), BF16),
            V((npsg, beams * cols // 256, 256), BF16),
            V((npsg, beams * cols // 256, 256), F32),
            V((2, half // npsg, cols), BF16),
            V((2, hb, half // npsg), BF16),
            V((2, npsg, hb, half // npsg), BF16),
            V((npsg, hb, half // npsg), BF16),
            D((16,)),
            D((6 + groups,)),
            D((6 + groups,)),
            D((2 * (npb - 1),)),
            D((2 * (npb - 1),)),
            D((npsg - 1,)),
            D((npsg - 1,)),
            D((npsg - 1,)),
            D((npsg - 1,)),
            D((npsg - 1,)),
            D((npsg - 1,)),
        ],
        compiler_params=pltpu.CompilerParams(
            collective_id=0, has_side_effects=True, vmem_limit_bytes=60 * 2**20
        ),
    )(
        tokens.reshape(rows, half), lengths, enc_gain.reshape(1, width), w_query, w_key, w_value, w_out,
        final_gain.reshape(1, width), cross_key, cross_value, beam_states.reshape(beams, width), parents,
        dec_gain.reshape(1, width), dec_query,
    )
    encoded, context = pl.pallas_call(
        writer,
        out_shape=(
            jax.ShapeDtypeStruct((rows, half), BF16),
            jax.ShapeDtypeStruct((beams, cols), F32),
        ),
        in_specs=[hbm, hbm],
        out_specs=(hbm, hbm),
        scratch_shapes=[V((rows, half), BF16), V((beams, cols), F32), D((9,)), D((9,))],
    )(encoded, context)
    return (
        encoded.reshape(questions, passages, plen, half),
        context.reshape(questions, beams, cols),
    )


def solution(mesh):
    in_specs = (
        P("pb", "psg", None, "tp"),
        P("pb", None),
        P(),
        P(None, "tp"),
        P(None, "tp"),
        P(None, "tp"),
        P("tp", None),
        P(),
        P(None, "tp"),
        P(None, "tp"),
        P("pb", None, None),
        P("pb", None),
        P(),
        P("pb", "tp"),
    )
    out_specs = (P("pb", "psg", None, "tp"), P("pb", None, "tp"))
    return jax.shard_map(
        per_device, mesh=mesh, in_specs=in_specs, out_specs=out_specs, check_vma=False
    )
```

```python
import functools
import math

import jax
import jax.numpy as jnp
from jax import lax
from jax.experimental import pallas as pl
from jax.experimental.pallas import tpu as pltpu
from jax.sharding import PartitionSpec as P

DH = 64
EPS = 1e-06
SCALE = 0.125
LOG2E = 1.4426950408889634
NEGATIVE = -1e30
MESH = pl.DeviceIdType.MESH
F32 = jnp.float32
BF16 = jnp.bfloat16


def nt_dot(a, b):
    return lax.dot_general(a, b, (((1,), (1,)), ((), ())), preferred_element_type=F32)


def nn_dot(a, b):
    return jnp.dot(a, b, preferred_element_type=F32)


def lane_fold(x):
    total = x[:, :128]
    for i in range(1, x.shape[1] // 128):
        total = total + x[:, i * 128 : (i + 1) * 128]
    return total


def body(
    sizes,
    tok_hbm, len_hbm, eg_hbm, wq_hbm, wk_hbm, wv_hbm, wo_hbm, fg_hbm, ck_hbm, cv_hbm, beam_hbm, par_hbm, dg_hbm, dec_hbm,
    enc_hbm, ctx_ref,
    tok, xl, xr, wbuf, wo, acc, qkv, att, attp, decw,
    sq, sqp, inv, gq, sc, scp, mix, mixp, bd, dn, dnr, dqp, dqr, stat, stats, ctf, ctp, cts, xs, ckb, gpart, gqa, gqp, len_ref, par_ref, eg_ref, fg_ref, dg_ref, beam_ref,
    lsem, tsend, trecv, psend, precv, ssend, srecv, csend, crecv, gsend, grecv, msem,
):
    npsg, npb = sizes
    enc = xl
    rows, half = tok.shape
    width = 2 * half
    cols = qkv.shape[2]
    heads = cols // DH
    beams = beam_ref.shape[0]
    hb = heads * beams
    plen = 256
    passages = rows // plen
    tp = lax.axis_index("tp")
    psg = lax.axis_index("psg")
    pb = lax.axis_index("pb")
    other = 1 - tp
    mine_f = pl.ds(pl.multiple_of(tp * half, half), half)
    peer_f = pl.ds(pl.multiple_of(other * half, half), half)

    small = (beam_hbm, beam_ref), (par_hbm, par_ref), (dg_hbm, dg_ref), (eg_hbm, eg_ref), (fg_hbm, fg_ref), (len_hbm, len_ref)
    small = [pltpu.make_async_copy(a, b, msem.at[i]) for i, (a, b) in enumerate(small)]
    for c in small:
        c.start()
    parts = 4
    prow = rows // parts
    copy_tok = [
        pltpu.make_async_copy(tok_hbm.at[pl.ds(i * prow, prow), :], tok.at[pl.ds(i * prow, prow), :], lsem.at[10 + i])
        for i in range(parts)
    ]
    for c in copy_tok:
        c.start()
    barrier = pltpu.get_barrier_semaphore()
    pl.semaphore_signal(barrier, inc=1, device_id={"tp": other}, device_id_type=MESH)

    def hello_psg(k, c):
        pl.semaphore_signal(barrier, inc=1, device_id={"psg": lax.rem(psg + k, npsg)}, device_id_type=MESH)
        return c

    lax.fori_loop(1, npsg, hello_psg, 0)
    for k in range(1, npb):
        pl.semaphore_signal(barrier, inc=1, device_id={"pb": lax.rem(pb + k, npb)}, device_id_type=MESH)

    w_hbm = (wq_hbm, wk_hbm, wv_hbm)
    copy_w = [[None, None] for _ in range(3)]
    for h, part in enumerate((mine_f, peer_f)):
        for w in range(3):
            copy_w[w][h] = pltpu.make_async_copy(w_hbm[w].at[part, :], wbuf.at[w, h], lsem.at[1 + 2 * w + h])
    copy_dec = pltpu.make_async_copy(dec_hbm, decw, lsem.at[7])
    copy_wo = pltpu.make_async_copy(wo_hbm.at[:, mine_f], wo.at[0], lsem.at[8])
    for w in range(3):
        copy_w[w][0].start()
    copy_dec.start()
    fc = half // npsg
    copy_ck = [
        pltpu.make_async_copy(ck_hbm.at[pl.ds(pl.multiple_of(c * half + psg * fc, fc), fc), :], ckb.at[f], lsem.at[14 + f])
        for f, c in enumerate((tp, other))
    ]
    for c in copy_ck:
        c.start()
    for w in range(3):
        copy_w[w][1].start()
    copy_wo.start()

    for c in small:
        c.wait()
    chosen = []
    for b in range(beams):
        row = jnp.zeros((1, width), F32)
        for c in range(beams):
            row = row + (par_ref[0, b] == c).astype(F32) * beam_ref[c : c + 1, :].astype(F32)
        chosen.append(row)
    depth = width // npb
    for b in range(beams):
        row = chosen[b]
        ms = jnp.sum(row * row, axis=-1, keepdims=True) * (1.0 / width) + EPS
        row = (row * lax.rsqrt(ms) * dg_ref[...]).astype(BF16).astype(F32)
        for j in range(npb):
            dn[j, b : b + 1, :] = row[:, j * depth : (j + 1) * depth]
    for j in range(npb):
        dn[j, beams:8, :] = jnp.zeros((8 - beams, depth), F32)

    blk = 32

    def scale_local(i, c):
        r = pl.ds(pl.multiple_of(i * blk, blk), blk)
        x = tok[r, :].astype(F32)
        sq[r, :] = lane_fold(x * x)
        xl[r, :] = (x * eg_ref[:, mine_f]).astype(BF16)
        return c

    for i in range(parts):
        copy_tok[i].wait()
        lax.fori_loop(i * prow // blk, (i + 1) * prow // blk, scale_local, 0)

    pl.semaphore_wait(barrier, npsg - 1 + npb - 1 + 1)

    def to_other(src, dst, i):
        return pltpu.make_async_remote_copy(
            src_ref=src, dst_ref=dst, send_sem=tsend.at[i], recv_sem=trecv.at[i],
            device_id={"tp": other}, device_id_type=MESH,
        )

    send_sq = to_other(sq, sqp, 0)
    send_tok = to_other(xl, xr, 1)
    send_wo = to_other(wo_hbm.at[:, peer_f], wo.at[1], 2)
    send_tok.start()
    send_sq.start()

    def to_pb(k, src, dst, base):
        to = lax.rem(pb + k, npb)
        return pltpu.make_async_remote_copy(
            src_ref=src.at[to], dst_ref=dst.at[pb], send_sem=psend.at[base + k - 1], recv_sem=precv.at[base + k - 1],
            device_id={"pb": to}, device_id_type=MESH,
        )

    side = math.isqrt(npsg)
    away = sorted(range(1, npsg), key=lambda k: -sum(min(c, side - c) for c in divmod(k, side)))

    def psg_at(k):
        return lax.rem(psg // side + k // side, side) * side + lax.rem(psg % side + k % side, side)

    def to_psg(k, src, dst, ss, rs):
        return pltpu.make_async_remote_copy(
            src_ref=src, dst_ref=dst, send_sem=ss.at[k - 1], recv_sem=rs.at[k - 1],
            device_id={"psg": psg_at(k)}, device_id_type=MESH,
        )

    send_dn = [to_pb(k, dn, dnr, 0) for k in range(1, npb)]
    for s in send_dn:
        s.start()
    dnr[pb] = dn[pb]

    nt = min(512, cols)
    for w in range(3):
        copy_w[w][0].wait()

        def first_half(j, c):
            t = slice(j * nt, j * nt + nt)
            acc[w, :, t] = nn_dot(xl[...], wbuf[w, 0, :, t])
            return c

        for j in range(cols // nt):
            first_half(j, 0)
        if w == 1:
            for s in send_dn:
                s.wait()
            copy_dec.wait()
            dqp[...] = nn_dot(dnr[...].reshape(npb * 8, depth).astype(BF16), decw[...]).reshape(npb, 8, cols)
            send_dq = [to_pb(k, dqp, dqr, npb - 1) for k in range(1, npb)]
            for s in send_dq:
                s.start()
            dqr[pb] = dqp[pb]

    copy_cv = [
        pltpu.make_async_copy(cv_hbm.at[mine_f, :], wbuf.at[0, 0], lsem.at[0]),
        pltpu.make_async_copy(cv_hbm.at[peer_f, :], wbuf.at[1, 0], lsem.at[9]),
    ]
    send_tok.wait()
    send_wo.start()
    send_sq.wait()

    def inverse(i, c):
        r = pl.ds(pl.multiple_of(i * blk, blk), blk)
        ms = jnp.sum(sq[r, :] + sqp[r, :], axis=-1, keepdims=True) * (1.0 / width) + EPS
        inv[r, :] = jnp.broadcast_to(lax.rsqrt(ms), (blk, 128))
        return c

    lax.fori_loop(0, rows // blk, inverse, 0)

    for w in range(3):
        copy_w[w][1].wait()

        def second_half(j, c):
            t = slice(j * nt, j * nt + nt)
            scale = jnp.concatenate([inv[...]] * (nt // 128), axis=1)
            qkv[w, :, t] = ((acc[w, :, t] + nn_dot(xr[...], wbuf[w, 1, :, t])) * scale).astype(BF16)
            return c

        for j in range(cols // nt):
            second_half(j, 0)
        if w == 0:
            copy_cv[0].start()
            copy_cv[1].start()
            for s in send_dq:
                s.wait()
            dq = dqr[0]
            for j in range(1, npb):
                dq = dq + dqr[j]
            dq = dq.astype(BF16).astype(F32)
            head_of = lax.broadcasted_iota(jnp.int32, (heads, cols), 1) // DH
            head_row = lax.broadcasted_iota(jnp.int32, (heads, cols), 0)
            for b in range(beams):
                bd[b * heads : (b + 1) * heads, :] = jnp.where(head_of == head_row, dq[b : b + 1, :], 0.0).astype(BF16)
            for f, c in enumerate((tp, other)):
                copy_ck[f].wait()
                gain = fg_ref[:, pl.ds(pl.multiple_of(c * half + psg * fc, fc), fc)]
                gpart[f] = (nt_dot(bd[...], ckb[f]) * gain).astype(BF16)

            for k in away:
                to_psg(k, gpart, gqa.at[:, psg], gsend, grecv).start()
            gqa[:, psg] = gpart[...]

    lane = lax.broadcasted_iota(jnp.int32, (plen, 128), 1)
    low = lane < DH
    slot = lax.broadcasted_iota(jnp.int32, (1, plen), 1)
    groups = cols // 256
    send_att = []
    for g in range(groups):
        for p in range(passages):
            key_live = slot < len_ref[0, psg * passages + p]
            r = slice(p * plen, (p + 1) * plen)
            for pair in range(2):
                t = slice(g * 256 + pair * 128, g * 256 + pair * 128 + 128)
                q = qkv[0, r, t]
                zero = jnp.zeros_like(q)
                q2 = jnp.concatenate([jnp.where(low, q, zero), jnp.where(low, zero, q)], axis=0)
                s = jnp.where(key_live, nt_dot(q2, qkv[1, r, t]), NEGATIVE)
                e = jnp.exp2((s - jnp.max(s, axis=-1, keepdims=True)) * (SCALE * LOG2E))
                den = jnp.sum(e, axis=-1, keepdims=True)
                o = nn_dot(e.astype(BF16), qkv[2, r, t]) / den
                att[r, t] = jnp.where(low, o[:plen], o[plen:]).astype(BF16)
        t = slice(g * 256, g * 256 + 256)
        s = to_other(att.at[:, t], attp.at[:, t], 3 + g)
        s.start()
        send_att.append(s)

    copy_wo.wait()

    def out_own(j, c):
        t = slice(j * nt, j * nt + nt)
        per = cols // nt
        acc[j // per, :, slice((j % per) * nt, (j % per) * nt + nt)] = nn_dot(att[...], wo[0, :, t])
        return c

    for j in range(half // nt):
        out_own(j, 0)
    mine_h = pl.ds(pl.multiple_of(tp * hb, hb), hb)
    peer_h = pl.ds(pl.multiple_of(other * hb, hb), hb)

    for k in away:
        to_psg(k, gpart, gqa.at[:, psg], gsend, grecv).wait()
    send_gq = to_other(gqa.at[1], gqp, 3 + groups)
    send_gq.start()
    for i in range(npsg):
        gq[mine_h, i * fc : (i + 1) * fc] = gqa[0, i]

    for s in send_att:
        s.wait()
    send_wo.wait()
    sq[...] = jnp.zeros_like(sq)

    def out_peer(j, c):
        t = slice(j * nt, j * nt + nt)
        per = cols // nt
        a = acc[j // per, :, slice((j % per) * nt, (j % per) * nt + nt)]
        e = (tok[:, t].astype(F32) + (a + nn_dot(attp[...], wo[1, :, t]))).astype(BF16)
        enc[:, t] = e
        wide = e.astype(F32)
        sq[...] += lane_fold(wide * wide)
        return c

    for j in range(half // nt):
        out_peer(j, 0)
    send_gq.wait()
    for i in range(npsg):
        gq[peer_h, i * fc : (i + 1) * fc] = gqp[i]
    sc[0 : 2 * hb, :] = nt_dot(gq[...], enc[...])
    copy_enc = pltpu.make_async_copy(enc, enc_hbm, lsem.at[13])
    sc[2 * hb : 2 * hb + 8, :] = jnp.broadcast_to(jnp.sum(jnp.transpose(sq[...]), axis=0, keepdims=True), (8, rows))
    send_sc = to_other(sc, scp, 4 + groups)
    send_sc.start()
    copy_enc.start()
    send_sc.wait()

    both = sc[...] + scp[...]
    x = both[2 * hb : 2 * hb + 1, :] * (1.0 / width) + EPS
    iv = lax.rsqrt(x)
    at = lax.broadcasted_iota(jnp.int32, (1, rows), 1)
    limit = jnp.zeros((1, rows), jnp.int32) + len_ref[0, psg * passages]
    for p in range(1, passages):
        limit = jnp.where(at >= p * plen, p * plen + len_ref[0, psg * passages + p], limit)
    live = at < limit
    s = jnp.where(live, both[0 : 2 * hb, :] * (iv * SCALE), NEGATIVE)
    peak = jnp.max(s, axis=1, keepdims=True)
    e = jnp.where(live, jnp.exp2((s - peak) * LOG2E), 0.0)
    wt = (e * iv).astype(BF16)
    total = jnp.sum(wt.astype(F32) * (x * iv), axis=1, keepdims=True)

    for j in range(half // nt):
        t = slice(j * nt, j * nt + nt)
        gain = fg_ref[:, pl.ds(pl.multiple_of(tp * half + j * nt, nt), nt)]
        mix[:, t] = (nn_dot(wt, enc[:, t]) * gain).astype(BF16)
    send_mix = to_other(mix.at[peer_h, :], mixp, 5 + groups)
    send_mix.start()
    first = lax.broadcasted_iota(jnp.int32, (2 * hb, 128), 1) == 0
    stat[...] = jnp.transpose(jnp.where(first, peak, total))[0:8, :]

    for k in away:
        to_psg(k, stat, stats.at[psg], ssend, srecv).start()
    stats[psg] = stat[...]


    ct = 256
    r_head = lax.rem(lax.broadcasted_iota(jnp.int32, (hb, ct), 0), heads)
    c_head = lax.broadcasted_iota(jnp.int32, (hb, ct), 1) // DH

    copy_cv[0].wait()
    for g in range(cols // ct):
        t = slice(g * ct, (g + 1) * ct)
        acc[0, 0:hb, t] = nn_dot(mix[mine_h, :], wbuf[0, 0, :, t])
    copy_cv[1].wait()
    send_mix.wait()
    for g in range(cols // ct):
        t = slice(g * ct, (g + 1) * ct)
        m = acc[0, 0:hb, t] + nn_dot(mixp[...], wbuf[1, 0, :, t])
        m = jnp.where(r_head == c_head + g * (ct // DH), m, 0.0)
        for b in range(beams):
            r = g * beams + b
            ctf[r : r + 1, :] = jnp.sum(m[b * heads : (b + 1) * heads], axis=0, keepdims=True)
    ctp[...] = ctf[...].astype(BF16)

    for k in away:
        to_psg(k, ctp, cts.at[psg], csend, crecv).start()
    cts[psg] = ctp[...]

    for k in away:
        to_psg(k, stat, stats.at[psg], ssend, srecv).wait()
    peaks = stats[:, 0:1, :]
    factor = jnp.exp2((peaks - jnp.max(peaks, axis=0, keepdims=True)) * LOG2E)
    factor = factor / jnp.sum(stats[:, 1:2, :] * factor, axis=0, keepdims=True)
    nr = beams * cols // ct
    per = ct // DH
    c_of = lax.broadcasted_iota(jnp.int32, (nr, 2 * hb), 1) - tp * hb
    r_of = lax.broadcasted_iota(jnp.int32, (nr, 2 * hb), 0)
    own = (c_of >= 0) & (c_of < hb) & (lax.div(c_of, heads) == lax.rem(r_of, beams))
    own = own & (lax.div(lax.rem(c_of, heads), per) == lax.div(r_of, beams))
    own = jnp.where(own, 1.0, 0.0)
    spread = (factor * own[None]).reshape(npsg * nr, 2 * hb)
    coarse = spread.astype(BF16)
    fine = (spread - coarse.astype(F32)).astype(BF16)
    one = lax.rem(lax.broadcasted_iota(jnp.int32, (2 * hb, ct), 0), per) == lax.broadcasted_iota(jnp.int32, (2 * hb, ct), 1) // DH
    one = jnp.where(one, 1.0, 0.0).astype(BF16)
    xs[...] = (nn_dot(coarse, one) + nn_dot(fine, one)).reshape(npsg, nr, ct)

    for k in away:
        to_psg(k, ctp, cts.at[psg], csend, crecv).wait()
    whole = jnp.sum(cts[...].astype(F32) * xs[...], axis=0)
    for g in range(cols // ct):
        ctx_ref[:, g * ct : (g + 1) * ct] = whole[g * beams : (g + 1) * beams, :]
    copy_enc.wait()


def writer(enc_hbm, ctx_hbm, enc_out, ctx_out, held, ctx, sem_in, sem_out):
    n = sem_in.shape[0] - 1
    rows = enc_hbm.shape[0] // n
    part = [pl.ds(i * rows, rows) for i in range(n)]
    ins = [pltpu.make_async_copy(enc_hbm.at[p, :], held.at[p, :], sem_in.at[i]) for i, p in enumerate(part)]
    ins.append(pltpu.make_async_copy(ctx_hbm, ctx, sem_in.at[n]))
    outs = [pltpu.make_async_copy(held.at[p, :], enc_out.at[p, :], sem_out.at[i]) for i, p in enumerate(part)]
    outs.append(pltpu.make_async_copy(ctx, ctx_out, sem_out.at[n]))
    for c in ins:
        c.start()
    for i in range(n + 1):
        ins[i].wait()
        outs[i].start()
    for c in outs:
        c.wait()


def per_device(
    tokens, lengths, enc_gain, w_query, w_key, w_value, w_out, final_gain, cross_key, cross_value,
    beam_states, parents, dec_gain, dec_query,
):
    questions, passages, plen, half = tokens.shape
    rows = questions * passages * plen
    cols = w_query.shape[1]
    heads = cols // DH
    beams = beam_states.shape[1]
    hb = heads * beams
    width = 2 * half
    npsg, npb = lax.axis_size("psg"), lax.axis_size("pb")
    groups = cols // 256
    vmem = pl.BlockSpec(memory_space=pltpu.VMEM)
    hbm = pl.BlockSpec(memory_space=pl.ANY)
    V, D = pltpu.VMEM, pltpu.SemaphoreType.DMA
    encoded, context = pl.pallas_call(
        functools.partial(body, (npsg, npb)),
        out_shape=(
            jax.ShapeDtypeStruct((rows, half), BF16),
            jax.ShapeDtypeStruct((beams, cols), F32),
        ),
        in_specs=[hbm] * 14,
        out_specs=(hbm, vmem),
        scratch_shapes=[
            V((rows, half), BF16),
            V((rows, half), BF16),
            V((rows, half), BF16),
            V((3, 2, half, cols), BF16),
            V((2, cols, half), BF16),
            V((3, rows, cols), F32),
            V((3, rows, cols), BF16),
            V((rows, cols), BF16),
            V((rows, cols), BF16),
            V((width // npb, cols), BF16),
            V((rows, 128), F32),
            V((rows, 128), F32),
            V((rows, 128), F32),
            V((2 * hb, half), BF16),
            V((2 * hb + 8, rows), F32),
            V((2 * hb + 8, rows), F32),
            V((2 * hb, half), BF16),
            V((hb, half), BF16),
            V((hb, cols), BF16),
            V((npb, 8, width // npb), F32),
            V((npb, 8, width // npb), F32),
            V((npb, 8, cols), F32),
            V((npb, 8, cols), F32),
            V((8, 2 * hb), F32),
            V((npsg, 8, 2 * hb), F32),
            V((beams * cols // 256, 256), F32),
            V((beams * cols // 256, 256), BF16),
            V((npsg, beams * cols // 256, 256), BF16),
            V((npsg, beams * cols // 256, 256), F32),
            V((2, half // npsg, cols), BF16),
            V((2, hb, half // npsg), BF16),
            V((2, npsg, hb, half // npsg), BF16),
            V((npsg, hb, half // npsg), BF16),
            pltpu.SMEM(lengths.shape, jnp.int32),
            pltpu.SMEM(parents.shape, jnp.int32),
            V((1, width), F32),
            V((1, width), F32),
            V((1, width), F32),
            V((beams, width), BF16),
            D((16,)),
            D((6 + groups,)),
            D((6 + groups,)),
            D((2 * (npb - 1),)),
            D((2 * (npb - 1),)),
            D((npsg - 1,)),
            D((npsg - 1,)),
            D((npsg - 1,)),
            D((npsg - 1,)),
            D((npsg - 1,)),
            D((npsg - 1,)),
            D((6,)),
        ],
        compiler_params=pltpu.CompilerParams(
            collective_id=0, has_side_effects=True, vmem_limit_bytes=60 * 2**20
        ),
    )(
        tokens.reshape(rows, half), lengths, enc_gain.reshape(1, width), w_query, w_key, w_value, w_out,
        final_gain.reshape(1, width), cross_key, cross_value, beam_states.reshape(beams, width), parents,
        dec_gain.reshape(1, width), dec_query,
    )
    encoded, context = pl.pallas_call(
        writer,
        out_shape=(
            jax.ShapeDtypeStruct((rows, half), BF16),
            jax.ShapeDtypeStruct((beams, cols), F32),
        ),
        in_specs=[hbm, hbm],
        out_specs=(hbm, hbm),
        scratch_shapes=[V((rows, half), BF16), V((beams, cols), F32), D((9,)), D((9,))],
    )(encoded, context)
    return (
        encoded.reshape(questions, passages, plen, half),
        context.reshape(questions, beams, cols),
    )


def solution(mesh):
    in_specs = (
        P("pb", "psg", None, "tp"),
        P("pb", None),
        P(),
        P(None, "tp"),
        P(None, "tp"),
        P(None, "tp"),
        P("tp", None),
        P(),
        P(None, "tp"),
        P(None, "tp"),
        P("pb", None, None),
        P("pb", None),
        P(),
        P("pb", "tp"),
    )
    out_specs = (P("pb", "psg", None, "tp"), P("pb", None, "tp"))
    return jax.shard_map(
        per_device, mesh=mesh, in_specs=in_specs, out_specs=out_specs, check_vma=False
    )
```

```python
import functools
import math

import jax
import jax.numpy as jnp
from jax import lax
from jax.experimental import pallas as pl
from jax.experimental.pallas import tpu as pltpu
from jax.sharding import PartitionSpec as P

DH = 64
EPS = 1e-06
SCALE = 0.125
LOG2E = 1.4426950408889634
NEGATIVE = -1e30
MESH = pl.DeviceIdType.MESH
F32 = jnp.float32
BF16 = jnp.bfloat16


def nt_dot(a, b):
    return lax.dot_general(a, b, (((1,), (1,)), ((), ())), preferred_element_type=F32)


def nn_dot(a, b):
    return jnp.dot(a, b, preferred_element_type=F32)


def lane_fold(x):
    total = x[:, :128]
    for i in range(1, x.shape[1] // 128):
        total = total + x[:, i * 128 : (i + 1) * 128]
    return total


def body(
    sizes,
    tok_hbm, len_hbm, eg_hbm, wq_hbm, wk_hbm, wv_hbm, wo_hbm, fg_hbm, ck_hbm, cv_hbm, beam_hbm, par_hbm, dg_hbm, dec_hbm,
    enc_hbm, ctx_ref,
    tok, xl, xr, wbuf, wo, acc, qkv, att, attp, decw,
    sq, sqp, inv, gq, sc, scp, mix, mixp, bd, dn, dnr, dqp, dqr, stat, stats, ctf, ctp, cts, xs, ckb, gpart, gqa, gqp, len_ref, par_ref, eg_ref, fg_ref, dg_ref, beam_ref,
    lsem, tsend, trecv, psend, precv, ssend, srecv, csend, crecv, gsend, grecv, msem,
):
    npsg, npb = sizes
    enc = xl
    rows, half = tok.shape
    width = 2 * half
    cols = qkv.shape[2]
    heads = cols // DH
    beams = beam_ref.shape[0]
    hb = heads * beams
    plen = 256
    passages = rows // plen
    tp = lax.axis_index("tp")
    psg = lax.axis_index("psg")
    pb = lax.axis_index("pb")
    other = 1 - tp
    mine_f = pl.ds(pl.multiple_of(tp * half, half), half)
    peer_f = pl.ds(pl.multiple_of(other * half, half), half)

    small = (beam_hbm, beam_ref), (par_hbm, par_ref), (dg_hbm, dg_ref), (eg_hbm, eg_ref), (fg_hbm, fg_ref), (len_hbm, len_ref)
    small = [pltpu.make_async_copy(a, b, msem.at[i]) for i, (a, b) in enumerate(small)]
    for c in small:
        c.start()
    parts = 4
    prow = rows // parts
    copy_tok = [
        pltpu.make_async_copy(tok_hbm.at[pl.ds(i * prow, prow), :], tok.at[pl.ds(i * prow, prow), :], lsem.at[10 + i])
        for i in range(parts)
    ]
    for c in copy_tok:
        c.start()
    barrier = pltpu.get_barrier_semaphore()
    pl.semaphore_signal(barrier, inc=1, device_id={"tp": other}, device_id_type=MESH)

    def hello_psg(k, c):
        pl.semaphore_signal(barrier, inc=1, device_id={"psg": lax.rem(psg + k, npsg)}, device_id_type=MESH)
        return c

    lax.fori_loop(1, npsg, hello_psg, 0)
    for k in range(1, npb):
        pl.semaphore_signal(barrier, inc=1, device_id={"pb": lax.rem(pb + k, npb)}, device_id_type=MESH)

    w_hbm = (wq_hbm, wk_hbm, wv_hbm)
    copy_w = [[None, None] for _ in range(3)]
    for h, part in enumerate((mine_f, peer_f)):
        for w in range(3):
            copy_w[w][h] = pltpu.make_async_copy(w_hbm[w].at[part, :], wbuf.at[w, h], lsem.at[1 + 2 * w + h])
    copy_dec = pltpu.make_async_copy(dec_hbm, decw, lsem.at[7])
    copy_wo = pltpu.make_async_copy(wo_hbm.at[:, mine_f], wo.at[0], lsem.at[8])
    for w in range(3):
        copy_w[w][0].start()
    copy_dec.start()
    fc = half // npsg
    copy_ck = [
        pltpu.make_async_copy(ck_hbm.at[pl.ds(pl.multiple_of(c * half + psg * fc, fc), fc), :], ckb.at[f], lsem.at[14 + f])
        for f, c in enumerate((tp, other))
    ]
    for c in copy_ck:
        c.start()
    for w in range(3):
        copy_w[w][1].start()
    copy_wo.start()

    for c in small:
        c.wait()
    chosen = []
    for b in range(beams):
        row = jnp.zeros((1, width), F32)
        for c in range(beams):
            row = row + (par_ref[0, b] == c).astype(F32) * beam_ref[c : c + 1, :].astype(F32)
        chosen.append(row)
    depth = width // npb
    for b in range(beams):
        row = chosen[b]
        ms = jnp.sum(row * row, axis=-1, keepdims=True) * (1.0 / width) + EPS
        row = (row * lax.rsqrt(ms) * dg_ref[...]).astype(BF16).astype(F32)
        for j in range(npb):
            dn[j, b : b + 1, :] = row[:, j * depth : (j + 1) * depth]
    for j in range(npb):
        dn[j, beams:8, :] = jnp.zeros((8 - beams, depth), F32)

    blk = 32

    def scale_local(i, c):
        r = pl.ds(pl.multiple_of(i * blk, blk), blk)
        x = tok[r, :].astype(F32)
        sq[r, :] = lane_fold(x * x)
        xl[r, :] = (x * eg_ref[:, mine_f]).astype(BF16)
        return c

    for i in range(parts):
        copy_tok[i].wait()
        lax.fori_loop(i * prow // blk, (i + 1) * prow // blk, scale_local, 0)

    pl.semaphore_wait(barrier, npsg - 1 + npb - 1 + 1)

    def to_other(src, dst, i):
        return pltpu.make_async_remote_copy(
            src_ref=src, dst_ref=dst, send_sem=tsend.at[i], recv_sem=trecv.at[i],
            device_id={"tp": other}, device_id_type=MESH,
        )

    send_sq = to_other(sq, sqp, 0)
    send_tok = to_other(xl, xr, 1)
    send_wo = to_other(wo_hbm.at[:, peer_f], wo.at[1], 2)
    send_tok.start()
    send_sq.start()

    def to_pb(k, src, dst, base):
        to = lax.rem(pb + k, npb)
        return pltpu.make_async_remote_copy(
            src_ref=src.at[to], dst_ref=dst.at[pb], send_sem=psend.at[base + k - 1], recv_sem=precv.at[base + k - 1],
            device_id={"pb": to}, device_id_type=MESH,
        )

    side = math.isqrt(npsg)
    away = sorted(range(1, npsg), key=lambda k: -sum(min(c, side - c) for c in divmod(k, side)))

    def psg_at(k):
        return lax.rem(psg // side + k // side, side) * side + lax.rem(psg % side + k % side, side)

    def to_psg(k, src, dst, ss, rs):
        return pltpu.make_async_remote_copy(
            src_ref=src, dst_ref=dst, send_sem=ss.at[k - 1], recv_sem=rs.at[k - 1],
            device_id={"psg": psg_at(k)}, device_id_type=MESH,
        )

    send_dn = [to_pb(k, dn, dnr, 0) for k in range(1, npb)]
    for s in send_dn:
        s.start()
    dnr[pb] = dn[pb]

    nt = min(512, cols)
    for w in range(3):
        copy_w[w][0].wait()

        def first_half(j, c):
            t = slice(j * nt, j * nt + nt)
            acc[w, :, t] = nn_dot(xl[...], wbuf[w, 0, :, t])
            return c

        for j in range(cols // nt):
            first_half(j, 0)
        if w == 1:
            for s in send_dn:
                s.wait()
            copy_dec.wait()
            dqp[...] = nn_dot(dnr[...].reshape(npb * 8, depth).astype(BF16), decw[...]).reshape(npb, 8, cols)
            send_dq = [to_pb(k, dqp, dqr, npb - 1) for k in range(1, npb)]
            for s in send_dq:
                s.start()
            dqr[pb] = dqp[pb]

    copy_cv = [
        pltpu.make_async_copy(cv_hbm.at[mine_f, :], wbuf.at[0, 0], lsem.at[0]),
        pltpu.make_async_copy(cv_hbm.at[peer_f, :], wbuf.at[1, 0], lsem.at[9]),
    ]
    send_tok.wait()
    send_wo.start()
    send_sq.wait()

    def inverse(i, c):
        r = pl.ds(pl.multiple_of(i * blk, blk), blk)
        ms = jnp.sum(sq[r, :] + sqp[r, :], axis=-1, keepdims=True) * (1.0 / width) + EPS
        inv[r, :] = jnp.broadcast_to(lax.rsqrt(ms), (blk, 128))
        return c

    lax.fori_loop(0, rows // blk, inverse, 0)

    for w in range(3):
        copy_w[w][1].wait()

        def second_half(j, c):
            t = slice(j * nt, j * nt + nt)
            scale = jnp.concatenate([inv[...]] * (nt // 128), axis=1)
            qkv[w, :, t] = ((acc[w, :, t] + nn_dot(xr[...], wbuf[w, 1, :, t])) * scale).astype(BF16)
            return c

        for j in range(cols // nt):
            second_half(j, 0)
        if w == 0:
            copy_cv[0].start()
            copy_cv[1].start()
            for s in send_dq:
                s.wait()
            dq = dqr[0]
            for j in range(1, npb):
                dq = dq + dqr[j]
            dq = dq.astype(BF16).astype(F32)
            head_of = lax.broadcasted_iota(jnp.int32, (heads, cols), 1) // DH
            head_row = lax.broadcasted_iota(jnp.int32, (heads, cols), 0)
            for b in range(beams):
                bd[b * heads : (b + 1) * heads, :] = jnp.where(head_of == head_row, dq[b : b + 1, :], 0.0).astype(BF16)
            for f, c in enumerate((tp, other)):
                copy_ck[f].wait()
                gain = fg_ref[:, pl.ds(pl.multiple_of(c * half + psg * fc, fc), fc)]
                gpart[f] = (nt_dot(bd[...], ckb[f]) * gain).astype(BF16)

            for k in away:
                to_psg(k, gpart, gqa.at[:, psg], gsend, grecv).start()
            gqa[:, psg] = gpart[...]

    lane = lax.broadcasted_iota(jnp.int32, (plen, 128), 1)
    low = lane < DH
    slot = lax.broadcasted_iota(jnp.int32, (1, plen), 1)
    groups = cols // 256
    send_att = []

    def logits(p, t):
        r = slice(p * plen, (p + 1) * plen)
        q = qkv[0, r, t]
        zero = jnp.zeros_like(q)
        q2 = jnp.concatenate([jnp.where(low, q, zero), jnp.where(low, zero, q)], axis=0)
        return nt_dot(q2, qkv[1, r, t])

    units = [(p, slice(h * 128, h * 128 + 128)) for g in range(groups) for p in range(passages) for h in (2 * g, 2 * g + 1)]
    following = logits(*units[0])

    def blend(i, e, den):
        p, t = units[i]
        r = slice(p * plen, (p + 1) * plen)
        o = nn_dot(e, qkv[2, r, t]) * den
        att[r, t] = jnp.where(low, o[:plen], o[plen:]).astype(BF16)
        if i % (2 * passages) == 2 * passages - 1:
            g = i // (2 * passages)
            t = slice(g * 256, g * 256 + 256)
            send = to_other(att.at[:, t], attp.at[:, t], 3 + g)
            send.start()
            send_att.append(send)

    before = None
    for i, (p, t) in enumerate(units):
        s = jnp.where(slot < len_ref[0, psg * passages + p], following, NEGATIVE)
        if i + 1 < len(units):
            following = logits(*units[i + 1])
        if before is not None:
            blend(i - 1, *before)
        e = jnp.exp2((s - jnp.max(s, axis=-1, keepdims=True)) * (SCALE * LOG2E))
        before = e.astype(BF16), 1.0 / jnp.sum(e, axis=-1, keepdims=True)
    blend(len(units) - 1, *before)

    copy_wo.wait()

    def out_own(j, c):
        t = slice(j * nt, j * nt + nt)
        per = cols // nt
        acc[j // per, :, slice((j % per) * nt, (j % per) * nt + nt)] = nn_dot(att[...], wo[0, :, t])
        return c

    for j in range(half // nt):
        out_own(j, 0)
    mine_h = pl.ds(pl.multiple_of(tp * hb, hb), hb)
    peer_h = pl.ds(pl.multiple_of(other * hb, hb), hb)

    for k in away:
        to_psg(k, gpart, gqa.at[:, psg], gsend, grecv).wait()
    send_gq = to_other(gqa.at[1], gqp, 3 + groups)
    send_gq.start()
    for i in range(npsg):
        gq[mine_h, i * fc : (i + 1) * fc] = gqa[0, i]

    for s in send_att:
        s.wait()
    send_wo.wait()
    sq[...] = jnp.zeros_like(sq)

    def out_peer(j, c):
        t = slice(j * nt, j * nt + nt)
        per = cols // nt
        a = acc[j // per, :, slice((j % per) * nt, (j % per) * nt + nt)]
        e = (tok[:, t].astype(F32) + (a + nn_dot(attp[...], wo[1, :, t]))).astype(BF16)
        enc[:, t] = e
        wide = e.astype(F32)
        sq[...] += lane_fold(wide * wide)
        return c

    for j in range(half // nt):
        out_peer(j, 0)
    send_gq.wait()
    for i in range(npsg):
        gq[peer_h, i * fc : (i + 1) * fc] = gqp[i]
    sc[0 : 2 * hb, :] = nt_dot(gq[...], enc[...])
    copy_enc = pltpu.make_async_copy(enc, enc_hbm, lsem.at[13])
    sc[2 * hb : 2 * hb + 8, :] = jnp.broadcast_to(jnp.sum(jnp.transpose(sq[...]), axis=0, keepdims=True), (8, rows))
    send_sc = to_other(sc, scp, 4 + groups)
    send_sc.start()
    copy_enc.start()
    send_sc.wait()

    both = sc[...] + scp[...]
    x = both[2 * hb : 2 * hb + 1, :] * (1.0 / width) + EPS
    iv = lax.rsqrt(x)
    at = lax.broadcasted_iota(jnp.int32, (1, rows), 1)
    limit = jnp.zeros((1, rows), jnp.int32) + len_ref[0, psg * passages]
    for p in range(1, passages):
        limit = jnp.where(at >= p * plen, p * plen + len_ref[0, psg * passages + p], limit)
    live = at < limit
    s = jnp.where(live, both[0 : 2 * hb, :] * (iv * SCALE), NEGATIVE)
    peak = jnp.max(s, axis=1, keepdims=True)
    e = jnp.where(live, jnp.exp2((s - peak) * LOG2E), 0.0)
    wt = (e * iv).astype(BF16)
    total = jnp.sum(wt.astype(F32) * (x * iv), axis=1, keepdims=True)

    for j in range(half // nt):
        t = slice(j * nt, j * nt + nt)
        gain = fg_ref[:, pl.ds(pl.multiple_of(tp * half + j * nt, nt), nt)]
        mix[:, t] = (nn_dot(wt, enc[:, t]) * gain).astype(BF16)
    send_mix = to_other(mix.at[peer_h, :], mixp, 5 + groups)
    send_mix.start()
    first = lax.broadcasted_iota(jnp.int32, (2 * hb, 128), 1) == 0
    stat[...] = jnp.transpose(jnp.where(first, peak, total))[0:8, :]

    for k in away:
        to_psg(k, stat, stats.at[psg], ssend, srecv).start()
    stats[psg] = stat[...]


    ct = 256
    r_head = lax.rem(lax.broadcasted_iota(jnp.int32, (hb, ct), 0), heads)
    c_head = lax.broadcasted_iota(jnp.int32, (hb, ct), 1) // DH

    copy_cv[0].wait()
    for g in range(cols // ct):
        t = slice(g * ct, (g + 1) * ct)
        acc[0, 0:hb, t] = nn_dot(mix[mine_h, :], wbuf[0, 0, :, t])
    copy_cv[1].wait()
    send_mix.wait()
    for g in range(cols // ct):
        t = slice(g * ct, (g + 1) * ct)
        m = acc[0, 0:hb, t] + nn_dot(mixp[...], wbuf[1, 0, :, t])
        m = jnp.where(r_head == c_head + g * (ct // DH), m, 0.0)
        for b in range(beams):
            r = g * beams + b
            ctf[r : r + 1, :] = jnp.sum(m[b * heads : (b + 1) * heads], axis=0, keepdims=True)
    ctp[...] = ctf[...].astype(BF16)

    for k in away:
        to_psg(k, ctp, cts.at[psg], csend, crecv).start()
    cts[psg] = ctp[...]

    for k in away:
        to_psg(k, stat, stats.at[psg], ssend, srecv).wait()
    peaks = stats[:, 0:1, :]
    factor = jnp.exp2((peaks - jnp.max(peaks, axis=0, keepdims=True)) * LOG2E)
    factor = factor / jnp.sum(stats[:, 1:2, :] * factor, axis=0, keepdims=True)
    nr = beams * cols // ct
    per = ct // DH
    c_of = lax.broadcasted_iota(jnp.int32, (nr, 2 * hb), 1) - tp * hb
    r_of = lax.broadcasted_iota(jnp.int32, (nr, 2 * hb), 0)
    own = (c_of >= 0) & (c_of < hb) & (lax.div(c_of, heads) == lax.rem(r_of, beams))
    own = own & (lax.div(lax.rem(c_of, heads), per) == lax.div(r_of, beams))
    own = jnp.where(own, 1.0, 0.0)
    spread = (factor * own[None]).reshape(npsg * nr, 2 * hb)
    coarse = spread.astype(BF16)
    fine = (spread - coarse.astype(F32)).astype(BF16)
    one = lax.rem(lax.broadcasted_iota(jnp.int32, (2 * hb, ct), 0), per) == lax.broadcasted_iota(jnp.int32, (2 * hb, ct), 1) // DH
    one = jnp.where(one, 1.0, 0.0).astype(BF16)
    xs[...] = (nn_dot(coarse, one) + nn_dot(fine, one)).reshape(npsg, nr, ct)

    for k in away:
        to_psg(k, ctp, cts.at[psg], csend, crecv).wait()
    whole = jnp.sum(cts[...].astype(F32) * xs[...], axis=0)
    for g in range(cols // ct):
        ctx_ref[:, g * ct : (g + 1) * ct] = whole[g * beams : (g + 1) * beams, :]
    copy_enc.wait()


def writer(enc_hbm, ctx_hbm, enc_out, ctx_out, held, ctx, sem_in, sem_out):
    n = sem_in.shape[0] - 1
    rows = enc_hbm.shape[0] // n
    part = [pl.ds(i * rows, rows) for i in range(n)]
    ins = [pltpu.make_async_copy(enc_hbm.at[p, :], held.at[p, :], sem_in.at[i]) for i, p in enumerate(part)]
    ins.append(pltpu.make_async_copy(ctx_hbm, ctx, sem_in.at[n]))
    outs = [pltpu.make_async_copy(held.at[p, :], enc_out.at[p, :], sem_out.at[i]) for i, p in enumerate(part)]
    outs.append(pltpu.make_async_copy(ctx, ctx_out, sem_out.at[n]))
    for c in ins:
        c.start()
    for i in range(n + 1):
        ins[i].wait()
        outs[i].start()
    for c in outs:
        c.wait()


def per_device(
    tokens, lengths, enc_gain, w_query, w_key, w_value, w_out, final_gain, cross_key, cross_value,
    beam_states, parents, dec_gain, dec_query,
):
    questions, passages, plen, half = tokens.shape
    rows = questions * passages * plen
    cols = w_query.shape[1]
    heads = cols // DH
    beams = beam_states.shape[1]
    hb = heads * beams
    width = 2 * half
    npsg, npb = lax.axis_size("psg"), lax.axis_size("pb")
    groups = cols // 256
    vmem = pl.BlockSpec(memory_space=pltpu.VMEM)
    hbm = pl.BlockSpec(memory_space=pl.ANY)
    V, D = pltpu.VMEM, pltpu.SemaphoreType.DMA
    encoded, context = pl.pallas_call(
        functools.partial(body, (npsg, npb)),
        out_shape=(
            jax.ShapeDtypeStruct((rows, half), BF16),
            jax.ShapeDtypeStruct((beams, cols), F32),
        ),
        in_specs=[hbm] * 14,
        out_specs=(hbm, vmem),
        scratch_shapes=[
            V((rows, half), BF16),
            V((rows, half), BF16),
            V((rows, half), BF16),
            V((3, 2, half, cols), BF16),
            V((2, cols, half), BF16),
            V((3, rows, cols), F32),
            V((3, rows, cols), BF16),
            V((rows, cols), BF16),
            V((rows, cols), BF16),
            V((width // npb, cols), BF16),
            V((rows, 128), F32),
            V((rows, 128), F32),
            V((rows, 128), F32),
            V((2 * hb, half), BF16),
            V((2 * hb + 8, rows), F32),
            V((2 * hb + 8, rows), F32),
            V((2 * hb, half), BF16),
            V((hb, half), BF16),
            V((hb, cols), BF16),
            V((npb, 8, width // npb), F32),
            V((npb, 8, width // npb), F32),
            V((npb, 8, cols), F32),
            V((npb, 8, cols), F32),
            V((8, 2 * hb), F32),
            V((npsg, 8, 2 * hb), F32),
            V((beams * cols // 256, 256), F32),
            V((beams * cols // 256, 256), BF16),
            V((npsg, beams * cols // 256, 256), BF16),
            V((npsg, beams * cols // 256, 256), F32),
            V((2, half // npsg, cols), BF16),
            V((2, hb, half // npsg), BF16),
            V((2, npsg, hb, half // npsg), BF16),
            V((npsg, hb, half // npsg), BF16),
            pltpu.SMEM(lengths.shape, jnp.int32),
            pltpu.SMEM(parents.shape, jnp.int32),
            V((1, width), F32),
            V((1, width), F32),
            V((1, width), F32),
            V((beams, width), BF16),
            D((16,)),
            D((6 + groups,)),
            D((6 + groups,)),
            D((2 * (npb - 1),)),
            D((2 * (npb - 1),)),
            D((npsg - 1,)),
            D((npsg - 1,)),
            D((npsg - 1,)),
            D((npsg - 1,)),
            D((npsg - 1,)),
            D((npsg - 1,)),
            D((6,)),
        ],
        compiler_params=pltpu.CompilerParams(
            collective_id=0, has_side_effects=True, vmem_limit_bytes=60 * 2**20
        ),
    )(
        tokens.reshape(rows, half), lengths, enc_gain.reshape(1, width), w_query, w_key, w_value, w_out,
        final_gain.reshape(1, width), cross_key, cross_value, beam_states.reshape(beams, width), parents,
        dec_gain.reshape(1, width), dec_query,
    )
    encoded, context = pl.pallas_call(
        writer,
        out_shape=(
            jax.ShapeDtypeStruct((rows, half), BF16),
            jax.ShapeDtypeStruct((beams, cols), F32),
        ),
        in_specs=[hbm, hbm],
        out_specs=(hbm, hbm),
        scratch_shapes=[V((rows, half), BF16), V((beams, cols), F32), D((9,)), D((9,))],
    )(encoded, context)
    return (
        encoded.reshape(questions, passages, plen, half),
        context.reshape(questions, beams, cols),
    )


def solution(mesh):
    in_specs = (
        P("pb", "psg", None, "tp"),
        P("pb", None),
        P(),
        P(None, "tp"),
        P(None, "tp"),
        P(None, "tp"),
        P("tp", None),
        P(),
        P(None, "tp"),
        P(None, "tp"),
        P("pb", None, None),
        P("pb", None),
        P(),
        P("pb", "tp"),
    )
    out_specs = (P("pb", "psg", None, "tp"), P("pb", None, "tp"))
    return jax.shard_map(
        per_device, mesh=mesh, in_specs=in_specs, out_specs=out_specs, check_vma=False
    )
```

```python
import functools
import math

import jax
import jax.numpy as jnp
from jax import lax
from jax.experimental import pallas as pl
from jax.experimental.pallas import tpu as pltpu
from jax.sharding import PartitionSpec as P

DH = 64
EPS = 1e-06
SCALE = 0.125
LOG2E = 1.4426950408889634
NEGATIVE = -1e30
MESH = pl.DeviceIdType.MESH
F32 = jnp.float32
BF16 = jnp.bfloat16


def nt_dot(a, b):
    return lax.dot_general(a, b, (((1,), (1,)), ((), ())), preferred_element_type=F32)


def nn_dot(a, b):
    return jnp.dot(a, b, preferred_element_type=F32)


def lane_fold(x):
    total = x[:, :128]
    for i in range(1, x.shape[1] // 128):
        total = total + x[:, i * 128 : (i + 1) * 128]
    return total


def body(
    sizes,
    tok_hbm, len_hbm, eg_hbm, wq_hbm, wk_hbm, wv_hbm, wo_hbm, fg_hbm, ck_hbm, cv_hbm, beam_hbm, par_hbm, dg_hbm, dec_hbm,
    enc_hbm, ctx_ref,
    tok, xl, xr, wbuf, wo, acc, qkv, att, attp, decw,
    sq, sqp, inv, gq, sc, scp, mix, mixp, bd, dn, dnr, dqp, dqr, stat, stats, ctf, ctp, cts, xs, ckb, gpart, gqa, gqp, len_ref, par_ref, eg_ref, fg_ref, dg_ref, beam_ref,
    lsem, tsend, trecv, psend, precv, ssend, srecv, csend, crecv, gsend, grecv, msem,
):
    npsg, npb = sizes
    enc = xl
    rows, half = tok.shape
    width = 2 * half
    cols = qkv.shape[2]
    heads = cols // DH
    beams = beam_ref.shape[0]
    hb = heads * beams
    plen = 256
    passages = rows // plen
    tp = lax.axis_index("tp")
    psg = lax.axis_index("psg")
    pb = lax.axis_index("pb")
    other = 1 - tp
    mine_f = pl.ds(pl.multiple_of(tp * half, half), half)
    peer_f = pl.ds(pl.multiple_of(other * half, half), half)

    small = (beam_hbm, beam_ref), (par_hbm, par_ref), (dg_hbm, dg_ref), (eg_hbm, eg_ref), (fg_hbm, fg_ref), (len_hbm, len_ref)
    small = [pltpu.make_async_copy(a, b, msem.at[i]) for i, (a, b) in enumerate(small)]
    for c in small:
        c.start()
    parts = 4
    prow = rows // parts
    copy_tok = [
        pltpu.make_async_copy(tok_hbm.at[pl.ds(i * prow, prow), :], tok.at[pl.ds(i * prow, prow), :], lsem.at[10 + i])
        for i in range(parts)
    ]
    for c in copy_tok:
        c.start()
    barrier = pltpu.get_barrier_semaphore()
    pl.semaphore_signal(barrier, inc=1, device_id={"tp": other}, device_id_type=MESH)

    def hello_psg(k, c):
        pl.semaphore_signal(barrier, inc=1, device_id={"psg": lax.rem(psg + k, npsg)}, device_id_type=MESH)
        return c

    lax.fori_loop(1, npsg, hello_psg, 0)
    for k in range(1, npb):
        pl.semaphore_signal(barrier, inc=1, device_id={"pb": lax.rem(pb + k, npb)}, device_id_type=MESH)

    w_hbm = (wq_hbm, wk_hbm, wv_hbm)
    copy_w = [[None, None] for _ in range(3)]
    for h, part in enumerate((mine_f, peer_f)):
        for w in range(3):
            copy_w[w][h] = pltpu.make_async_copy(w_hbm[w].at[part, :], wbuf.at[w, h], lsem.at[1 + 2 * w + h])
    copy_dec = pltpu.make_async_copy(dec_hbm, decw, lsem.at[7])
    copy_wo = pltpu.make_async_copy(wo_hbm.at[:, mine_f], wo.at[0], lsem.at[8])
    for w in range(3):
        copy_w[w][0].start()
    copy_dec.start()
    fc = half // npsg
    copy_ck = [
        pltpu.make_async_copy(ck_hbm.at[pl.ds(pl.multiple_of(c * half + psg * fc, fc), fc), :], ckb.at[f], lsem.at[14 + f])
        for f, c in enumerate((tp, other))
    ]
    for c in copy_ck:
        c.start()
    for w in range(3):
        copy_w[w][1].start()
    copy_wo.start()

    for c in small:
        c.wait()
    chosen = []
    for b in range(beams):
        row = jnp.zeros((1, width), F32)
        for c in range(beams):
            row = row + (par_ref[0, b] == c).astype(F32) * beam_ref[c : c + 1, :].astype(F32)
        chosen.append(row)
    depth = width // npb
    for b in range(beams):
        row = chosen[b]
        ms = jnp.sum(row * row, axis=-1, keepdims=True) * (1.0 / width) + EPS
        row = (row * lax.rsqrt(ms) * dg_ref[...]).astype(BF16).astype(F32)
        for j in range(npb):
            dn[j, b : b + 1, :] = row[:, j * depth : (j + 1) * depth]
    for j in range(npb):
        dn[j, beams:8, :] = jnp.zeros((8 - beams, depth), F32)

    blk = 32

    def scale_local(i, c):
        r = pl.ds(pl.multiple_of(i * blk, blk), blk)
        x = tok[r, :].astype(F32)
        sq[r, :] = lane_fold(x * x)
        xl[r, :] = (x * eg_ref[:, mine_f]).astype(BF16)
        return c

    for i in range(parts):
        copy_tok[i].wait()
        lax.fori_loop(i * prow // blk, (i + 1) * prow // blk, scale_local, 0)

    pl.semaphore_wait(barrier, npsg - 1 + npb - 1 + 1)

    def to_other(src, dst, i):
        return pltpu.make_async_remote_copy(
            src_ref=src, dst_ref=dst, send_sem=tsend.at[i], recv_sem=trecv.at[i],
            device_id={"tp": other}, device_id_type=MESH,
        )

    send_sq = to_other(sq, sqp, 0)
    send_tok = to_other(xl, xr, 1)
    send_wo = to_other(wo_hbm.at[:, peer_f], wo.at[1], 2)
    send_tok.start()
    send_sq.start()

    def to_pb(k, src, dst, base):
        to = lax.rem(pb + k, npb)
        return pltpu.make_async_remote_copy(
            src_ref=src.at[to], dst_ref=dst.at[pb], send_sem=psend.at[base + k - 1], recv_sem=precv.at[base + k - 1],
            device_id={"pb": to}, device_id_type=MESH,
        )

    side = math.isqrt(npsg)
    away = sorted(range(1, npsg), key=lambda k: -sum(min(c, side - c) for c in divmod(k, side)))

    def psg_at(k):
        return lax.rem(psg // side + k // side, side) * side + lax.rem(psg % side + k % side, side)

    def to_psg(k, src, dst, ss, rs):
        return pltpu.make_async_remote_copy(
            src_ref=src, dst_ref=dst, send_sem=ss.at[k - 1], recv_sem=rs.at[k - 1],
            device_id={"psg": psg_at(k)}, device_id_type=MESH,
        )

    send_dn = [to_pb(k, dn, dnr, 0) for k in range(1, npb)]
    for s in send_dn:
        s.start()
    dnr[pb] = dn[pb]

    nt = min(512, cols)
    for w in range(3):
        copy_w[w][0].wait()

        def first_half(j, c):
            t = slice(j * nt, j * nt + nt)
            acc[w, :, t] = nn_dot(xl[...], wbuf[w, 0, :, t])
            return c

        for j in range(cols // nt):
            first_half(j, 0)
        if w == 1:
            for s in send_dn:
                s.wait()
            copy_dec.wait()
            dqp[...] = nn_dot(dnr[...].reshape(npb * 8, depth).astype(BF16), decw[...]).reshape(npb, 8, cols)
            send_dq = [to_pb(k, dqp, dqr, npb - 1) for k in range(1, npb)]
            for s in send_dq:
                s.start()
            dqr[pb] = dqp[pb]

    copy_cv = [
        pltpu.make_async_copy(cv_hbm.at[mine_f, :], wbuf.at[0, 0], lsem.at[0]),
        pltpu.make_async_copy(cv_hbm.at[peer_f, :], wbuf.at[1, 0], lsem.at[9]),
    ]
    send_tok.wait()
    send_wo.start()
    send_sq.wait()

    def inverse(i, c):
        r = pl.ds(pl.multiple_of(i * blk, blk), blk)
        ms = jnp.sum(sq[r, :] + sqp[r, :], axis=-1, keepdims=True) * (1.0 / width) + EPS
        inv[r, :] = jnp.broadcast_to(lax.rsqrt(ms), (blk, 128))
        return c

    lax.fori_loop(0, rows // blk, inverse, 0)

    for w in range(3):
        copy_w[w][1].wait()

        def second_half(j, c):
            t = slice(j * nt, j * nt + nt)
            scale = jnp.concatenate([inv[...]] * (nt // 128), axis=1)
            qkv[w, :, t] = ((acc[w, :, t] + nn_dot(xr[...], wbuf[w, 1, :, t])) * scale).astype(BF16)
            return c

        for j in range(cols // nt):
            second_half(j, 0)
        if w == 0:
            copy_cv[0].start()
            copy_cv[1].start()
            for s in send_dq:
                s.wait()
            dq = dqr[0]
            for j in range(1, npb):
                dq = dq + dqr[j]
            dq = dq.astype(BF16).astype(F32)
            head_of = lax.broadcasted_iota(jnp.int32, (heads, cols), 1) // DH
            head_row = lax.broadcasted_iota(jnp.int32, (heads, cols), 0)
            for b in range(beams):
                bd[b * heads : (b + 1) * heads, :] = jnp.where(head_of == head_row, dq[b : b + 1, :], 0.0).astype(BF16)
            for f, c in enumerate((tp, other)):
                copy_ck[f].wait()
                gain = fg_ref[:, pl.ds(pl.multiple_of(c * half + psg * fc, fc), fc)]
                gpart[f] = (nt_dot(bd[...], ckb[f]) * gain).astype(BF16)

            for k in away:
                to_psg(k, gpart, gqa.at[:, psg], gsend, grecv).start()
            gqa[:, psg] = gpart[...]

    lane = lax.broadcasted_iota(jnp.int32, (plen, 128), 1)
    low = lane < DH
    slot = lax.broadcasted_iota(jnp.int32, (1, plen), 1)
    groups = cols // 256
    send_att = []

    def logits(p, t):
        r = slice(p * plen, (p + 1) * plen)
        q = qkv[0, r, t]
        zero = jnp.zeros_like(q)
        q2 = jnp.concatenate([jnp.where(low, q, zero), jnp.where(low, zero, q)], axis=0)
        return nt_dot(q2, qkv[1, r, t])

    units = [(p, slice(h * 128, h * 128 + 128)) for g in range(groups) for p in range(passages) for h in (2 * g, 2 * g + 1)]
    following = logits(*units[0])

    def blend(i, e):
        p, t = units[i]
        r = slice(p * plen, (p + 1) * plen)
        v = qkv[2, r, t]
        one = jnp.ones_like(v)
        o0 = nn_dot(e[:plen], jnp.where(low, v, one))
        o1 = nn_dot(e[plen:], jnp.where(low, one, v))
        den = pltpu.roll(jnp.where(low, o1, o0), DH, 1)
        att[r, t] = (jnp.where(low, o0, o1) / den).astype(BF16)
        if i % (2 * passages) == 2 * passages - 1:
            g = i // (2 * passages)
            t = slice(g * 256, g * 256 + 256)
            send = to_other(att.at[:, t], attp.at[:, t], 3 + g)
            send.start()
            send_att.append(send)

    before = None
    for i, (p, t) in enumerate(units):
        s = jnp.where(slot < len_ref[0, psg * passages + p], following, NEGATIVE)
        if i + 1 < len(units):
            following = logits(*units[i + 1])
        if before is not None:
            blend(i - 1, before)
        e = jnp.exp2((s - jnp.max(s, axis=-1, keepdims=True)) * (SCALE * LOG2E))
        before = e.astype(BF16)
    blend(len(units) - 1, before)

    copy_wo.wait()

    def out_own(j, c):
        t = slice(j * nt, j * nt + nt)
        per = cols // nt
        acc[j // per, :, slice((j % per) * nt, (j % per) * nt + nt)] = nn_dot(att[...], wo[0, :, t])
        return c

    for j in range(half // nt):
        out_own(j, 0)
    mine_h = pl.ds(pl.multiple_of(tp * hb, hb), hb)
    peer_h = pl.ds(pl.multiple_of(other * hb, hb), hb)

    for k in away:
        to_psg(k, gpart, gqa.at[:, psg], gsend, grecv).wait()
    send_gq = to_other(gqa.at[1], gqp, 3 + groups)
    send_gq.start()
    for i in range(npsg):
        gq[mine_h, i * fc : (i + 1) * fc] = gqa[0, i]

    for s in send_att:
        s.wait()
    send_wo.wait()
    sq[...] = jnp.zeros_like(sq)

    def out_peer(j, c):
        t = slice(j * nt, j * nt + nt)
        per = cols // nt
        a = acc[j // per, :, slice((j % per) * nt, (j % per) * nt + nt)]
        e = (tok[:, t].astype(F32) + (a + nn_dot(attp[...], wo[1, :, t]))).astype(BF16)
        enc[:, t] = e
        wide = e.astype(F32)
        sq[...] += lane_fold(wide * wide)
        return c

    for j in range(half // nt):
        out_peer(j, 0)
    send_gq.wait()
    for i in range(npsg):
        gq[peer_h, i * fc : (i + 1) * fc] = gqp[i]
    sc[0 : 2 * hb, :] = nt_dot(gq[...], enc[...])
    copy_enc = pltpu.make_async_copy(enc, enc_hbm, lsem.at[13])
    sc[2 * hb : 2 * hb + 8, :] = jnp.broadcast_to(jnp.sum(jnp.transpose(sq[...]), axis=0, keepdims=True), (8, rows))
    send_sc = to_other(sc, scp, 4 + groups)
    send_sc.start()
    copy_enc.start()
    send_sc.wait()

    both = sc[...] + scp[...]
    x = both[2 * hb : 2 * hb + 1, :] * (1.0 / width) + EPS
    iv = lax.rsqrt(x)
    at = lax.broadcasted_iota(jnp.int32, (1, rows), 1)
    limit = jnp.zeros((1, rows), jnp.int32) + len_ref[0, psg * passages]
    for p in range(1, passages):
        limit = jnp.where(at >= p * plen, p * plen + len_ref[0, psg * passages + p], limit)
    live = at < limit
    s = jnp.where(live, both[0 : 2 * hb, :] * (iv * SCALE), NEGATIVE)
    peak = jnp.max(s, axis=1, keepdims=True)
    e = jnp.where(live, jnp.exp2((s - peak) * LOG2E), 0.0)
    wt = (e * iv).astype(BF16)
    total = jnp.sum(wt.astype(F32) * (x * iv), axis=1, keepdims=True)

    for j in range(half // nt):
        t = slice(j * nt, j * nt + nt)
        gain = fg_ref[:, pl.ds(pl.multiple_of(tp * half + j * nt, nt), nt)]
        mix[:, t] = (nn_dot(wt, enc[:, t]) * gain).astype(BF16)
    send_mix = to_other(mix.at[peer_h, :], mixp, 5 + groups)
    send_mix.start()
    first = lax.broadcasted_iota(jnp.int32, (2 * hb, 128), 1) == 0
    stat[...] = jnp.transpose(jnp.where(first, peak, total))[0:8, :]

    for k in away:
        to_psg(k, stat, stats.at[psg], ssend, srecv).start()
    stats[psg] = stat[...]


    ct = 256
    r_head = lax.rem(lax.broadcasted_iota(jnp.int32, (hb, ct), 0), heads)
    c_head = lax.broadcasted_iota(jnp.int32, (hb, ct), 1) // DH

    copy_cv[0].wait()
    for g in range(cols // ct):
        t = slice(g * ct, (g + 1) * ct)
        acc[0, 0:hb, t] = nn_dot(mix[mine_h, :], wbuf[0, 0, :, t])
    copy_cv[1].wait()
    send_mix.wait()
    for g in range(cols // ct):
        t = slice(g * ct, (g + 1) * ct)
        m = acc[0, 0:hb, t] + nn_dot(mixp[...], wbuf[1, 0, :, t])
        m = jnp.where(r_head == c_head + g * (ct // DH), m, 0.0)
        for b in range(beams):
            r = g * beams + b
            ctf[r : r + 1, :] = jnp.sum(m[b * heads : (b + 1) * heads], axis=0, keepdims=True)
    ctp[...] = ctf[...].astype(BF16)

    for k in away:
        to_psg(k, ctp, cts.at[psg], csend, crecv).start()
    cts[psg] = ctp[...]

    for k in away:
        to_psg(k, stat, stats.at[psg], ssend, srecv).wait()
    peaks = stats[:, 0:1, :]
    factor = jnp.exp2((peaks - jnp.max(peaks, axis=0, keepdims=True)) * LOG2E)
    factor = factor / jnp.sum(stats[:, 1:2, :] * factor, axis=0, keepdims=True)
    nr = beams * cols // ct
    per = ct // DH
    c_of = lax.broadcasted_iota(jnp.int32, (nr, 2 * hb), 1) - tp * hb
    r_of = lax.broadcasted_iota(jnp.int32, (nr, 2 * hb), 0)
    own = (c_of >= 0) & (c_of < hb) & (lax.div(c_of, heads) == lax.rem(r_of, beams))
    own = own & (lax.div(lax.rem(c_of, heads), per) == lax.div(r_of, beams))
    own = jnp.where(own, 1.0, 0.0)
    spread = (factor * own[None]).reshape(npsg * nr, 2 * hb)
    coarse = spread.astype(BF16)
    fine = (spread - coarse.astype(F32)).astype(BF16)
    one = lax.rem(lax.broadcasted_iota(jnp.int32, (2 * hb, ct), 0), per) == lax.broadcasted_iota(jnp.int32, (2 * hb, ct), 1) // DH
    one = jnp.where(one, 1.0, 0.0).astype(BF16)
    xs[...] = (nn_dot(coarse, one) + nn_dot(fine, one)).reshape(npsg, nr, ct)

    for k in away:
        to_psg(k, ctp, cts.at[psg], csend, crecv).wait()
    whole = jnp.sum(cts[...].astype(F32) * xs[...], axis=0)
    for g in range(cols // ct):
        ctx_ref[:, g * ct : (g + 1) * ct] = whole[g * beams : (g + 1) * beams, :]
    copy_enc.wait()


def writer(enc_hbm, ctx_hbm, enc_out, ctx_out, held, ctx, sem_in, sem_out):
    n = sem_in.shape[0] - 1
    rows = enc_hbm.shape[0] // n
    part = [pl.ds(i * rows, rows) for i in range(n)]
    ins = [pltpu.make_async_copy(enc_hbm.at[p, :], held.at[p, :], sem_in.at[i]) for i, p in enumerate(part)]
    ins.append(pltpu.make_async_copy(ctx_hbm, ctx, sem_in.at[n]))
    outs = [pltpu.make_async_copy(held.at[p, :], enc_out.at[p, :], sem_out.at[i]) for i, p in enumerate(part)]
    outs.append(pltpu.make_async_copy(ctx, ctx_out, sem_out.at[n]))
    for c in ins:
        c.start()
    for i in range(n + 1):
        ins[i].wait()
        outs[i].start()
    for c in outs:
        c.wait()


def per_device(
    tokens, lengths, enc_gain, w_query, w_key, w_value, w_out, final_gain, cross_key, cross_value,
    beam_states, parents, dec_gain, dec_query,
):
    questions, passages, plen, half = tokens.shape
    rows = questions * passages * plen
    cols = w_query.shape[1]
    heads = cols // DH
    beams = beam_states.shape[1]
    hb = heads * beams
    width = 2 * half
    npsg, npb = lax.axis_size("psg"), lax.axis_size("pb")
    groups = cols // 256
    vmem = pl.BlockSpec(memory_space=pltpu.VMEM)
    hbm = pl.BlockSpec(memory_space=pl.ANY)
    V, D = pltpu.VMEM, pltpu.SemaphoreType.DMA
    encoded, context = pl.pallas_call(
        functools.partial(body, (npsg, npb)),
        out_shape=(
            jax.ShapeDtypeStruct((rows, half), BF16),
            jax.ShapeDtypeStruct((beams, cols), F32),
        ),
        in_specs=[hbm] * 14,
        out_specs=(hbm, vmem),
        scratch_shapes=[
            V((rows, half), BF16),
            V((rows, half), BF16),
            V((rows, half), BF16),
            V((3, 2, half, cols), BF16),
            V((2, cols, half), BF16),
            V((3, rows, cols), F32),
            V((3, rows, cols), BF16),
            V((rows, cols), BF16),
            V((rows, cols), BF16),
            V((width // npb, cols), BF16),
            V((rows, 128), F32),
            V((rows, 128), F32),
            V((rows, 128), F32),
            V((2 * hb, half), BF16),
            V((2 * hb + 8, rows), F32),
            V((2 * hb + 8, rows), F32),
            V((2 * hb, half), BF16),
            V((hb, half), BF16),
            V((hb, cols), BF16),
            V((npb, 8, width // npb), F32),
            V((npb, 8, width // npb), F32),
            V((npb, 8, cols), F32),
            V((npb, 8, cols), F32),
            V((8, 2 * hb), F32),
            V((npsg, 8, 2 * hb), F32),
            V((beams * cols // 256, 256), F32),
            V((beams * cols // 256, 256), BF16),
            V((npsg, beams * cols // 256, 256), BF16),
            V((npsg, beams * cols // 256, 256), F32),
            V((2, half // npsg, cols), BF16),
            V((2, hb, half // npsg), BF16),
            V((2, npsg, hb, half // npsg), BF16),
            V((npsg, hb, half // npsg), BF16),
            pltpu.SMEM(lengths.shape, jnp.int32),
            pltpu.SMEM(parents.shape, jnp.int32),
            V((1, width), F32),
            V((1, width), F32),
            V((1, width), F32),
            V((beams, width), BF16),
            D((16,)),
            D((6 + groups,)),
            D((6 + groups,)),
            D((2 * (npb - 1),)),
            D((2 * (npb - 1),)),
            D((npsg - 1,)),
            D((npsg - 1,)),
            D((npsg - 1,)),
            D((npsg - 1,)),
            D((npsg - 1,)),
            D((npsg - 1,)),
            D((6,)),
        ],
        compiler_params=pltpu.CompilerParams(
            collective_id=0, has_side_effects=True, vmem_limit_bytes=60 * 2**20
        ),
    )(
        tokens.reshape(rows, half), lengths, enc_gain.reshape(1, width), w_query, w_key, w_value, w_out,
        final_gain.reshape(1, width), cross_key, cross_value, beam_states.reshape(beams, width), parents,
        dec_gain.reshape(1, width), dec_query,
    )
    encoded, context = pl.pallas_call(
        writer,
        out_shape=(
            jax.ShapeDtypeStruct((rows, half), BF16),
            jax.ShapeDtypeStruct((beams, cols), F32),
        ),
        in_specs=[hbm, hbm],
        out_specs=(hbm, hbm),
        scratch_shapes=[V((rows, half), BF16), V((beams, cols), F32), D((9,)), D((9,))],
    )(encoded, context)
    return (
        encoded.reshape(questions, passages, plen, half),
        context.reshape(questions, beams, cols),
    )


def solution(mesh):
    in_specs = (
        P("pb", "psg", None, "tp"),
        P("pb", None),
        P(),
        P(None, "tp"),
        P(None, "tp"),
        P(None, "tp"),
        P("tp", None),
        P(),
        P(None, "tp"),
        P(None, "tp"),
        P("pb", None, None),
        P("pb", None),
        P(),
        P("pb", "tp"),
    )
    out_specs = (P("pb", "psg", None, "tp"), P("pb", None, "tp"))
    return jax.shard_map(
        per_device, mesh=mesh, in_specs=in_specs, out_specs=out_specs, check_vma=False
    )
```
